128 devices in a mesh: ctx: 32 (over y, z, core), ch: 4 (over x).
Axes of the slice: x: 4, y: 4, z: 4, core: 2. Of those that a mesh axis runs over, the one named last changes fastest.
Arguments:
- tokens: bfloat16 [32768, 4096], P('ctx', 'ch'), may hold values from -6 to 6
- w_input: bfloat16 [2, 4096, 4096], P(None, None, 'ch'), may hold values from -0.09375 to 0.09375
- w_output: bfloat16 [4096, 4096], P('ctx', 'ch'), may hold values from -0.09375 to 0.09375
- bias_update: float32 [4096], P('ch'), may hold values from -14 to 1
- bias_cand: float32 [4096], P('ch'), may hold values from -1 to 1
- recur_gain: float32 [4096], P('ch'), may hold values from -0.95 to 0.95
- start_state: float32 [4096], P('ch'), may hold values from -1 to 1
Outputs:
- mixed: bfloat16 [32768, 4096], P('ctx', 'ch')
The draws below stay inside these ranges and needn't reach their ends.
All inputs are finite; a program needn't handle non-finite values.
Results may differ from the reference program's by a relative error of at most 0.005.
Values may be sent and summed in bfloat16 or wider, within the bound.
A program may use at most 128 MiB of HBM per device.

```python
import math
import jax
import jax.numpy as jnp
from jax import lax

D = 4096
ITERS = 2
LENGTH = 32768


def draw_bias_update(key, part):
    pick_key = jax.random.fold_in(key, 11)
    slow_key = jax.random.fold_in(key, 12)
    fast_key = jax.random.fold_in(key, 13)
    slow_share = 0.5
    is_slow = jax.random.bernoulli(pick_key, slow_share, (D,))
    span = jnp.log(jnp.float32(LENGTH))
    slow_rate = jax.random.uniform(slow_key, (D,), jnp.float32, -3.0, 0.5) - span
    fast_rate = jax.random.uniform(fast_key, (D,), jnp.float32, -4.0, 1.0)
    return jnp.where(is_slow, slow_rate, fast_rate)


def block_levels(stream_key, shape, shards, least, top_value):
    level = 1.0
    for dim, shards_of in shards:
        heights = jax.random.uniform(jax.random.fold_in(jax.random.fold_in(stream_key, 6), dim), (shards_of,), jnp.float32, least / len(shards), top_value / len(shards))
        level = level * jnp.repeat(jnp.exp(heights), shape[dim] // shards_of).reshape((-1,) + (1,) * (len(shape) - 1 - dim))
    return level


def noise(rng, dims, width, reach, cuts=(), dtype=jnp.bfloat16):
    factor_of = block_levels(rng, dims, cuts, -0.22, 0.18) if cuts else 1.0
    drawn = jax.random.normal(rng, dims, jnp.float32) * width * factor_of
    return jnp.minimum(jnp.maximum(drawn, -reach), reach).astype(dtype)


def setup_inputs(seed: int = 0) -> dict:
    key_list = jax.random.split(jax.random.key(seed), 8)
    return {
        "tokens": noise(key_list[0], (LENGTH, D), 1.0, 6.0, ((0, 32), (1, 4))),
        "w_input": noise(key_list[1], (2, D, D), D ** -0.5, 0.09375, ((2, 4),)),
        "w_output": noise(key_list[2], (D, D), D ** -0.5, 0.09375, ((0, 32), (1, 4))),
        "bias_update": draw_bias_update(jax.random.fold_in(key_list[7], 71), 0),
        "bias_cand": jnp.clip(jax.random.uniform(key_list[4], (D,), jnp.float32, -1.0, 1.0) * block_levels(key_list[4], (D,), ((0, 4),), -0.4, 0.0), -1.0, 1.0),
        "recur_gain": jnp.clip(jax.random.uniform(key_list[5], (D,), jnp.float32, -0.95, 0.95) * block_levels(key_list[5], (D,), ((0, 4),), -0.4, 0.0), -0.95, 0.95),
        "start_state": jnp.clip(jax.random.uniform(key_list[6], (D,), jnp.float32, -1.0, 1.0) * block_levels(key_list[6], (D,), ((0, 4),), -0.4, 0.0), -1.0, 1.0),
    }


def advance(state_vec, pair_in):
    new_state = pair_in[0] * state_vec + pair_in[1]
    return new_state, new_state


def reference(tokens, w_input, w_output, bias_update, bias_cand, recur_gain, start_state):
    block_width = math.gcd(D, 256)
    blocks = D // block_width
    w_blocks = w_input.reshape(2, D, blocks, block_width).transpose(2, 0, 1, 3)

    def solve_block(pieces):
        w_cols, bias_gate, bias_value, gain_row, start_row = pieces
        update_pre = (jnp.dot(tokens, w_cols[0], preferred_element_type=jnp.float32) + bias_gate).astype(jnp.bfloat16)
        cand_pre = (jnp.dot(tokens, w_cols[1], preferred_element_type=jnp.float32) + bias_value).astype(jnp.bfloat16)
        update_pre, cand_pre = lax.optimization_barrier((update_pre, cand_pre))
        update = jax.nn.sigmoid(update_pre.astype(jnp.float32))
        candidate = cand_pre.astype(jnp.float32)
        trajectory = jnp.zeros((LENGTH, block_width), jnp.float32)
        for iteration in range(ITERS):
            previous = jnp.concatenate([start_row[None, :], trajectory[:-1]], axis=0)
            squashed = jnp.tanh(candidate + gain_row * previous)
            mapped = (1.0 - update) * previous + update * squashed
            slopes = (1.0 - update) + update * gain_row * (1.0 - squashed * squashed)
            offsets = mapped - slopes * previous
            ignored, trajectory = lax.scan(advance, start_row, (slopes, offsets))
        return trajectory.astype(jnp.bfloat16)

    pieces = (w_blocks, bias_update.reshape(blocks, block_width), bias_cand.reshape(blocks, block_width),
              recur_gain.reshape(blocks, block_width), start_state.reshape(blocks, block_width))
    states = lax.map(solve_block, pieces)
    states = states.transpose(1, 0, 2).reshape(LENGTH, D)
    return jnp.dot(states, w_output, preferred_element_type=jnp.float32).astype(jnp.bfloat16)
```

```python
import functools

import jax
import jax.numpy as jnp
from jax import lax
from jax.experimental import pallas as pl
from jax.experimental.pallas import tpu as pltpu
from jax.sharding import PartitionSpec as P

LANES = 128
SUBS = 8
CHUNKS = 4
TILE = 256
BLOCK = 16
F32 = jnp.float32
BF16 = jnp.bfloat16


def mul(index, size):
    return pl.multiple_of(index * size, size)


def kernel(
    n_ctx, n_ch, rows, width,
    tok, w_in, w_out, bias_u, bias_c, gain_ref, start_ref, out,
    x, w, wo, ubuf, cbuf, sbuf, obuf, stage, msg, inbox,
    own_send, own_recv, fwd_send, fwd_recv,
    wo_send, wo_recv, pair_send, pair_recv,
    x_sem, w_sem, wo_sem, out_sem, msg_send, msg_recv, free,
):
    me = lax.axis_index("ctx")
    col = lax.axis_index("ch")
    right = lax.rem(col + 1, n_ch)
    left = lax.rem(col + n_ch - 1, n_ch)
    far = lax.rem(col + 2, n_ch)
    sources = (col, left, right, far)
    chunk = rows // CHUNKS
    half = chunk // 2
    wo_rows = w_out.shape[0]
    pairs = n_ctx // 2
    core = lax.rem(me, 2)
    mate = me + 1 - 2 * core
    chip = lax.div(me, 2)
    tiles = width // TILE

    barrier = pltpu.get_barrier_semaphore()
    for neighbour in (left, right):
        pl.semaphore_signal(barrier, inc=1, device_id={"ch": neighbour}, device_id_type=pl.DeviceIdType.MESH)

    def greet(j, carry):
        pl.semaphore_signal(
            barrier, inc=1, device_id={"ctx": lax.rem(me + j, n_ctx)}, device_id_type=pl.DeviceIdType.MESH
        )
        return carry

    lax.fori_loop(1, n_ctx, greet, 0)
    pl.semaphore_wait(barrier, n_ctx + 1)

    def own_copy(source, way, k):
        peer = (right, left)[way]
        return pltpu.make_async_remote_copy(
            src_ref=source.at[pl.ds(mul(k, chunk), chunk), :],
            dst_ref=x.at[1 + way, pl.ds(mul(k, chunk), chunk), :],
            send_sem=own_send.at[way, k],
            recv_sem=own_recv.at[way, k],
            device_id={"ch": peer},
            device_id_type=pl.DeviceIdType.MESH,
        )

    def fwd_copy(way, k):
        peer = (right, left)[way]
        at = pl.ds(pl.multiple_of(k * chunk + way * half, half), half)
        return pltpu.make_async_remote_copy(
            src_ref=x.at[1 + way, at, :],
            dst_ref=x.at[3, at, :],
            send_sem=fwd_send.at[way, k],
            recv_sem=fwd_recv.at[way, k],
            device_id={"ch": peer},
            device_id_type=pl.DeviceIdType.MESH,
        )

    def send_own(source, k):
        own_copy(source, 0, k).start()
        own_copy(source, 1, k).start()

    def pass_on(k):
        for way in range(2):
            own_copy(x.at[0], way, k).wait_recv()
            fwd_copy(way, k).start()

    def await_far(k):
        for way in range(2):
            fwd_copy(way, k).wait_recv()

    def finish_sends(k, carry):
        for way in range(2):
            own_copy(x.at[0], way, k).wait_send()
            fwd_copy(way, k).wait_send()
        return carry

    def start_own(k, carry):
        send_own(tok, k)
        return carry

    lax.fori_loop(0, CHUNKS, start_own, 0)

    x_copy = pltpu.make_async_copy(tok, x.at[0], x_sem)
    x_copy.start()

    def w_copy(slot):
        return pltpu.make_async_copy(
            w_in.at[:, pl.ds(mul(sources[slot], width), width), :], w.at[slot], w_sem.at[slot]
        )

    for slot in range(4):
        w_copy(slot).start()

    def wo_at(owner):
        return wo.at[pl.ds(mul(owner, wo_rows), wo_rows), :]

    wo_copy = pltpu.make_async_copy(w_out, wo_at(me), wo_sem)
    wo_copy.start()

    def wo_spread(j, owner_chip):
        return pltpu.make_async_remote_copy(
            src_ref=w_out,
            dst_ref=wo_at(owner_chip * 2 + core),
            send_sem=wo_send.at[j],
            recv_sem=wo_recv.at[owner_chip],
            device_id={"ctx": j * 2 + core},
            device_id_type=pl.DeviceIdType.MESH,
        )

    def pair_copy(j, of_core):
        return pltpu.make_async_remote_copy(
            src_ref=wo_at(j * 2 + of_core),
            dst_ref=wo_at(j * 2 + of_core),
            send_sem=pair_send.at[j],
            recv_sem=pair_recv.at[j],
            device_id={"ctx": mate},
            device_id_type=pl.DeviceIdType.MESH,
        )

    def start_spread(i, carry):
        wo_spread(lax.rem(chip + i, pairs), chip).start()
        return carry

    lax.fori_loop(1, pairs, start_spread, 0)
    wo_copy.wait()
    pair_copy(chip, core).start()

    def pair_on(i, carry):
        j = lax.rem(chip + pairs - i, pairs)
        wo_spread(j, j).wait_recv()
        pair_copy(j, core).start()
        return carry

    def pair_wait(j, carry):
        pair_copy(j, 1 - core).wait_recv()
        return carry

    def pair_finish(j, carry):
        pair_copy(j, core).wait_send()
        return carry

    def spread_finish(i, carry):
        wo_spread(lax.rem(chip + i, pairs), chip).wait_send()
        return carry

    def natural(k, tile):
        return pl.ds(pl.multiple_of(k * chunk * SUBS + tile * chunk, chunk), chunk)

    def near_gates(k, carry):
        pass_on(k)
        at = pl.ds(mul(k, chunk), chunk)

        def tile_step(n, inner):
            cols = pl.ds(mul(n, TILE), TILE)
            for gate, target in ((0, sbuf), (1, obuf)):
                total = jnp.dot(x[0, at, :], w[0, gate, :, cols], preferred_element_type=F32)
                total += jnp.dot(x[1, at, :], w[1, gate, :, cols], preferred_element_type=F32)
                total += jnp.dot(x[2, at, :], w[2, gate, :, cols], preferred_element_type=F32)
                for p in range(TILE // LANES):
                    target[natural(k, n * (TILE // LANES) + p), :] = total[:, p * LANES : (p + 1) * LANES]
            return inner

        lax.fori_loop(0, tiles, tile_step, 0)
        return carry

    x_copy.wait()
    for slot in range(4):
        w_copy(slot).wait()
    lax.fori_loop(0, CHUNKS, near_gates, 0)

    gain = gain_ref[...]
    start = start_ref[...]
    first_prev = jnp.where(me == 0, start, jnp.zeros_like(start))

    def far_gates(k):
        await_far(k)
        at = pl.ds(mul(k, chunk), chunk)

        def tile_step(n, inner):
            cols = pl.ds(mul(n, TILE), TILE)
            for gate, base, bias, target in ((0, sbuf, bias_u, ubuf), (1, obuf, bias_c, cbuf)):
                total = jnp.dot(x[3, at, :], w[3, gate, :, cols], preferred_element_type=F32)
                for p in range(TILE // LANES):
                    tile = n * (TILE // LANES) + p
                    part = total[:, p * LANES : (p + 1) * LANES] + base[natural(k, tile), :]
                    part = part + bias[:, pl.ds(mul(tile, LANES), LANES)]
                    part = part.astype(BF16).astype(F32)
                    if gate == 0:
                        part = 1.0 / (1.0 + jnp.exp(-part))
                    target[pl.ds(k * chunk * SUBS + tile, chunk, stride=SUBS), :] = part
            return inner

        lax.fori_loop(0, tiles, tile_step, 0)

    def token(ref, t):
        return ref[pl.ds(mul(t, SUBS), SUBS), :]

    def put(ref, t, value):
        ref[pl.ds(mul(t, SUBS), SUBS), :] = value

    def first_block(b, carry):
        acc_s, acc_o = carry
        base = b * BLOCK
        lead = jnp.where(b == 0, first_prev, jnp.zeros_like(start))
        for i in range(BLOCK):
            update = token(ubuf, base + i)
            cand = token(cbuf, base + i)
            keep = 1.0 - update
            if i == 0:
                squashed = jnp.tanh(cand + gain * lead)
                slope = keep + update * gain * (1.0 - squashed * squashed)
                offset = keep * lead + update * squashed - slope * lead
            else:
                squashed = jnp.tanh(cand)
                slope = keep + update * gain * (1.0 - squashed * squashed)
                offset = update * squashed
            put(sbuf, base + i, slope)
            put(obuf, base + i, offset)
            acc_o = slope * acc_o + offset
            acc_s = slope * acc_s
        return acc_s, acc_o

    blocks = chunk // BLOCK

    def far_step(k, carry):
        far_gates(k)
        return lax.fori_loop(k * blocks, (k + 1) * blocks, first_block, carry)

    ident = (jnp.ones_like(start), jnp.zeros_like(start))
    carry = lax.fori_loop(0, CHUNKS - 1, far_step, ident)
    lax.fori_loop(1, pairs, pair_on, 0)
    carry = far_step(CHUNKS - 1, carry)

    def message(stage_no, source, target):
        return pltpu.make_async_remote_copy(
            src_ref=msg.at[stage_no],
            dst_ref=inbox.at[stage_no, source],
            send_sem=msg_send.at[target],
            recv_sem=msg_recv.at[stage_no, source],
            device_id={"ctx": target},
            device_id_type=pl.DeviceIdType.MESH,
        )

    def send_maps(stage_no, maps):
        msg[stage_no, pl.ds(0, SUBS), :] = maps[0]
        msg[stage_no, pl.ds(SUBS, SUBS), :] = maps[1]

        def post(d, c):
            message(stage_no, me, d).start()
            return c

        lax.fori_loop(me + 1, n_ctx, post, 0)

    def entering(stage_no):
        def take(d, h):
            message(stage_no, d, d).wait_recv()
            return inbox[stage_no, d, pl.ds(0, SUBS), :] * h + inbox[stage_no, d, pl.ds(SUBS, SUBS), :]

        return lax.fori_loop(0, me, take, start)

    def posted(stage_no):
        def done(d, c):
            message(stage_no, me, d).wait_send()
            return c

        lax.fori_loop(me + 1, n_ctx, done, 0)

    send_maps(0, carry)
    lax.fori_loop(0, CHUNKS, finish_sends, 0)
    for neighbour in (left, right):
        pl.semaphore_signal(free, inc=1, device_id={"ch": neighbour}, device_id_type=pl.DeviceIdType.MESH)
    state = entering(0)
    posted(0)

    def second_block(b, carry):
        h, acc_s, acc_o = carry
        base = b * BLOCK
        for i in range(BLOCK):
            prev = h
            h = token(sbuf, base + i) * h + token(obuf, base + i)
            update = token(ubuf, base + i)
            cand = token(cbuf, base + i)
            keep = 1.0 - update
            squashed = jnp.tanh(cand + gain * prev)
            slope = keep + update * gain * (1.0 - squashed * squashed)
            offset = keep * prev + update * squashed - slope * prev
            put(sbuf, base + i, slope)
            put(obuf, base + i, offset)
            acc_o = slope * acc_o + offset
            acc_s = slope * acc_s
        return h, acc_s, acc_o

    final = lax.fori_loop(0, CHUNKS * blocks, second_block, (state,) + ident)
    send_maps(1, final[1:])
    state = entering(1)
    posted(1)
    pl.semaphore_wait(free, 2)

    def last_block(b, h):
        base = b * BLOCK
        for i in range(BLOCK):
            h = token(sbuf, base + i) * h + token(obuf, base + i)
            put(ubuf, base + i, h)
        return h

    def last_step(k, h):
        h = lax.fori_loop(k * blocks, (k + 1) * blocks, last_block, h)
        at = pl.ds(mul(k, chunk), chunk)
        for tile in range(SUBS):
            values = ubuf[pl.ds(k * chunk * SUBS + tile, chunk, stride=SUBS), :]
            x[0, at, tile * LANES : (tile + 1) * LANES] = values.astype(BF16)
        send_own(x.at[0], k)
        return h

    lax.fori_loop(0, CHUNKS, last_step, state)
    lax.fori_loop(0, pairs, pair_wait, 0)

    def w_part(slot, cols):
        return wo[pl.ds(mul(sources[slot], width), width), cols]

    def near_out(k, carry):
        pass_on(k)
        at = pl.ds(mul(k, chunk), chunk)

        def tile_step(n, inner):
            cols = pl.ds(mul(n, TILE), TILE)
            total = jnp.dot(x[0, at, :], w_part(0, cols), preferred_element_type=F32)
            total += jnp.dot(x[1, at, :], w_part(1, cols), preferred_element_type=F32)
            total += jnp.dot(x[2, at, :], w_part(2, cols), preferred_element_type=F32)
            for p in range(TILE // LANES):
                cbuf[natural(k, n * (TILE // LANES) + p), :] = total[:, p * LANES : (p + 1) * LANES]
            return inner

        lax.fori_loop(0, tiles, tile_step, 0)
        return carry

    lax.fori_loop(0, CHUNKS, near_out, 0)

    def out_copy(k):
        at = pl.ds(mul(k, chunk), chunk)
        return pltpu.make_async_copy(stage.at[at, :], out.at[at, :], out_sem.at[k])

    def far_out(k, carry):
        await_far(k)
        at = pl.ds(mul(k, chunk), chunk)

        def tile_step(n, inner):
            cols = pl.ds(mul(n, TILE), TILE)
            total = jnp.dot(x[3, at, :], w_part(3, cols), preferred_element_type=F32)
            for p in range(TILE // LANES):
                tile = n * (TILE // LANES) + p
                part = total[:, p * LANES : (p + 1) * LANES] + cbuf[natural(k, tile), :]
                stage[at, pl.ds(mul(tile, LANES), LANES)] = part.astype(BF16)
            return inner

        lax.fori_loop(0, tiles, tile_step, 0)
        out_copy(k).start()
        return carry

    lax.fori_loop(0, CHUNKS, far_out, 0)
    lax.fori_loop(0, CHUNKS, finish_sends, 0)
    lax.fori_loop(1, pairs, spread_finish, 0)
    lax.fori_loop(0, pairs, pair_finish, 0)

    def out_wait(k, carry):
        out_copy(k).wait()
        return carry

    lax.fori_loop(0, CHUNKS, out_wait, 0)


def on_device(tokens, w_input, w_output, bias_update, bias_cand, recur_gain, start_state):
    rows, width = tokens.shape
    n_ctx = lax.axis_size("ctx")
    n_ch = lax.axis_size("ch")
    any_spec = pl.BlockSpec(memory_space=pl.ANY)
    vmem_spec = pl.BlockSpec(memory_space=pltpu.VMEM)
    dma = pltpu.SemaphoreType.DMA
    return pl.pallas_call(
        functools.partial(kernel, n_ctx, n_ch, rows, width),
        out_shape=jax.ShapeDtypeStruct((rows, width), BF16),
        in_specs=[any_spec] * 3 + [vmem_spec] * 4,
        out_specs=any_spec,
        scratch_shapes=[
            pltpu.VMEM((4, rows, width), BF16),
            pltpu.VMEM((4, 2, width, width), BF16),
            pltpu.VMEM((n_ch * width, width), BF16),
            pltpu.VMEM((rows * SUBS, LANES), F32),
            pltpu.VMEM((rows * SUBS, LANES), F32),
            pltpu.VMEM((rows * SUBS, LANES), F32),
            pltpu.VMEM((rows * SUBS, LANES), F32),
            pltpu.VMEM((rows, width), BF16),
            pltpu.VMEM((2, 2 * SUBS, LANES), F32),
            pltpu.VMEM((2, n_ctx, 2 * SUBS, LANES), F32),
            dma((2, CHUNKS)),
            dma((2, CHUNKS)),
            dma((2, CHUNKS)),
            dma((2, CHUNKS)),
            dma((n_ctx // 2,)),
            dma((n_ctx // 2,)),
            dma((n_ctx // 2,)),
            dma((n_ctx // 2,)),
            dma,
            dma((4,)),
            dma,
            dma((CHUNKS,)),
            dma((n_ctx,)),
            dma((2, n_ctx)),
            pltpu.SemaphoreType.REGULAR,
        ],
        compiler_params=pltpu.CompilerParams(
            collective_id=0, has_side_effects=True, vmem_limit_bytes=60 * 1024 * 1024
        ),
        cost_estimate=pl.CostEstimate(
            flops=6 * rows * width * width * n_ch,
            bytes_accessed=2 * (2 * rows * width + 3 * width * width * n_ch),
            transcendentals=4 * rows * width,
        ),
    )(
        tokens,
        w_input,
        w_output,
        bias_update.reshape(1, width),
        bias_cand.reshape(1, width),
        recur_gain.reshape(SUBS, LANES),
        start_state.reshape(SUBS, LANES),
    )


def solution(mesh):
    return jax.shard_map(
        on_device,
        mesh=mesh,
        in_specs=(
            P("ctx", "ch"),
            P(None, None, "ch"),
            P("ctx", "ch"),
            P("ch"),
            P("ch"),
            P("ch"),
            P("ch"),
        ),
        out_specs=P("ctx", "ch"),
        check_vma=False,
    )
```

```python
import functools

import jax
import jax.numpy as jnp
from jax import lax
from jax.experimental import pallas as pl
from jax.experimental.pallas import tpu as pltpu
from jax.sharding import PartitionSpec as P

LANES = 128
CHUNKS = 4
TILE = 256
BLOCK = 16
SPAN = 4
F32 = jnp.float32
BF16 = jnp.bfloat16


def mul(index, size):
    return pl.multiple_of(index * size, size)


def kernel(
    n_ctx, n_ch, rows, width,
    tok, w_in, w_out, bias_u, bias_c, gain_ref, start_ref, out,
    x, w, wo, ubuf, cbuf, sbuf, obuf, msg, inbox,
    own_send, own_recv, fwd_send, fwd_recv,
    line_send, line_recv, hop_send, hop_recv,
    row_send, row_recv, turn_send, turn_recv,
    mate_send, mate_recv, give_send, give_recv, cross_send, cross_recv,
    x_sem, w_sem, wo_sem, out_sem, msg_send, msg_recv, free,
):
    subs = width // LANES
    size = min(TILE, width)
    me = lax.axis_index("ctx")
    col = lax.axis_index("ch")
    pair = col + 1 - 2 * lax.rem(col, 2)
    across = n_ch - 1 - col
    far = lax.rem(col + 2, n_ch)
    sources = (col, pair, across, far)
    mine = lax.rem(lax.div(col + 1, 2), 2)
    chunk = rows // CHUNKS
    part_rows = chunk // 2
    pair_share = chunk * 7 // 16 // 16 * 16 or chunk // 2
    wo_rows = w_out.shape[0]
    chips = n_ctx // 2
    core = lax.rem(me, 2)
    mate = me + 1 - 2 * core
    tiles = width // size
    y_at = lax.div(me, 2 * SPAN)
    z_at = lax.rem(lax.div(me, 2), SPAN)

    def spot(f, first, second):
        first = lax.rem(first + SPAN, SPAN)
        second = lax.rem(second + SPAN, SPAN)
        y, z = (first, second) if f == 0 else (second, first)
        return (y * SPAN + z) * 2 + core

    barrier = pltpu.get_barrier_semaphore()
    for neighbour in (pair, across):
        pl.semaphore_signal(barrier, inc=1, device_id={"ch": neighbour}, device_id_type=pl.DeviceIdType.MESH)
    around = [spot(0, y_at + 1, z_at), spot(0, y_at - 1, z_at), spot(0, y_at, z_at + 1), spot(0, y_at, z_at - 1), mate]
    for neighbour in around:
        pl.semaphore_signal(barrier, inc=1, device_id={"ctx": neighbour}, device_id_type=pl.DeviceIdType.MESH)
    pl.semaphore_wait(barrier, 2 + len(around))

    def wo_piece(owner, low, count):
        return wo.at[:, pl.ds(pl.multiple_of(owner * wo_rows + low, 16), count), :]

    wo_copy = pltpu.make_async_copy(w_out, wo.at[0, pl.ds(mul(me, wo_rows), wo_rows), :], wo_sem)
    wo_copy.start()
    cross = pltpu.make_async_remote_copy(
        src_ref=w_out,
        dst_ref=wo.at[1, pl.ds(mul(me, wo_rows), wo_rows), :],
        send_sem=cross_send,
        recv_sem=cross_recv,
        device_id={"ch": pair},
        device_id_type=pl.DeviceIdType.MESH,
    )
    cross.start()

    def own_copy(source, way, k):
        peer = (pair, across)[way]
        return pltpu.make_async_remote_copy(
            src_ref=source.at[pl.ds(mul(k, chunk), chunk), :],
            dst_ref=x.at[1 + way, pl.ds(mul(k, chunk), chunk), :],
            send_sem=own_send.at[way, k],
            recv_sem=own_recv.at[way, k],
            device_id={"ch": peer},
            device_id_type=pl.DeviceIdType.MESH,
        )

    fwd_rows = (chunk - pair_share, pair_share)

    def fwd_copy(way, k):
        peer = (across, pair)[way]
        at = pl.ds(pl.multiple_of(k * chunk + way * fwd_rows[0], 16), fwd_rows[way])
        return pltpu.make_async_remote_copy(
            src_ref=x.at[1 + way, at, :],
            dst_ref=x.at[3, at, :],
            send_sem=fwd_send.at[way, k],
            recv_sem=fwd_recv.at[way, k],
            device_id={"ch": peer},
            device_id_type=pl.DeviceIdType.MESH,
        )

    def send_own(source, k):
        own_copy(source, 0, k).start()
        own_copy(source, 1, k).start()

    def pass_on(k):
        for way in range(2):
            own_copy(x.at[0], way, k).wait_recv()
            fwd_copy(way, k).start()

    def await_far(k):
        for way in range(2):
            fwd_copy(way, k).wait_recv()

    def finish_sends(k, carry):
        for way in range(2):
            own_copy(x.at[0], way, k).wait_send()
            fwd_copy(way, k).wait_send()
        return carry

    def start_own(k, carry):
        send_own(tok, k)
        return carry

    lax.fori_loop(0, CHUNKS, start_own, 0)

    x_copy = pltpu.make_async_copy(tok, x.at[0], x_sem)
    x_copy.start()

    def w_copy(slot):
        return pltpu.make_async_copy(
            w_in.at[:, pl.ds(mul(sources[slot], width), width), :], w.at[slot], w_sem.at[slot]
        )

    for slot in range(4):
        w_copy(slot).start()

    half = wo_rows // 2
    quarter = half // 2

    def line_copy(f, way):
        a, b = (y_at, z_at) if f == 0 else (z_at, y_at)
        step = 1 - 2 * way
        piece = wo_piece(me, f * half, half)
        return pltpu.make_async_remote_copy(
            src_ref=piece, dst_ref=piece,
            send_sem=line_send.at[f, way], recv_sem=line_recv.at[f, way],
            device_id={"ctx": spot(f, a + step, b)}, device_id_type=pl.DeviceIdType.MESH,
        )

    def hop_copy(f, way):
        a, b = (y_at, z_at) if f == 0 else (z_at, y_at)
        step = 1 - 2 * way
        piece = wo_piece(spot(f, a - step, b), f * half + way * quarter, quarter)
        return pltpu.make_async_remote_copy(
            src_ref=piece, dst_ref=piece,
            send_sem=hop_send.at[f, way], recv_sem=hop_recv.at[f, way],
            device_id={"ctx": spot(f, a + step, b)}, device_id_type=pl.DeviceIdType.MESH,
        )

    def row_copy(f, j, way):
        a, b = (y_at, z_at) if f == 0 else (z_at, y_at)
        step = 1 - 2 * way
        piece = wo_piece(spot(f, a + j, b), f * half, half)
        return pltpu.make_async_remote_copy(
            src_ref=piece, dst_ref=piece,
            send_sem=row_send.at[f, j, way], recv_sem=row_recv.at[f, j, way],
            device_id={"ctx": spot(f, a, b + step)}, device_id_type=pl.DeviceIdType.MESH,
        )

    def turn_copy(f, j, way):
        a, b = (y_at, z_at) if f == 0 else (z_at, y_at)
        step = 1 - 2 * way
        piece = wo_piece(spot(f, a + j, b - step), f * half + way * quarter, quarter)
        return pltpu.make_async_remote_copy(
            src_ref=piece, dst_ref=piece,
            send_sem=turn_send.at[f, j, way], recv_sem=turn_recv.at[f, j, way],
            device_id={"ctx": spot(f, a, b + step)}, device_id_type=pl.DeviceIdType.MESH,
        )

    def mate_copy(j, of_core):
        piece = wo_piece(j * 2 + of_core, 0, wo_rows)
        return pltpu.make_async_remote_copy(
            src_ref=piece, dst_ref=piece,
            send_sem=mate_send.at[j], recv_sem=mate_recv.at[j],
            device_id={"ctx": mate}, device_id_type=pl.DeviceIdType.MESH,
        )

    both = [(f, way) for f in range(2) for way in range(2)]

    def begin_lines():
        wo_copy.wait()
        cross.wait_recv()
        for f, way in both:
            line_copy(f, way).start()
        for f, way in both:
            row_copy(f, 0, way).start()

    def begin_hops():
        for f, way in both:
            line_copy(f, way).wait_recv()
            hop_copy(f, way).start()
        for j in (1, 3):
            for f, way in both:
                row_copy(f, j, way).start()

    def begin_last_row():
        for f, way in both:
            hop_copy(f, way).wait_recv()
        for f, way in both:
            row_copy(f, 2, way).start()

    def turn(j):
        for f, way in both:
            row_copy(f, j, way).wait_recv()
            turn_copy(f, j, way).start()

    def begin_mates():
        for j in range(SPAN):
            for f, way in both:
                turn_copy(f, j, way).wait_recv()

        def start_mate(j, carry):
            mate_copy(j, core).start()
            return carry

        lax.fori_loop(0, chips, start_mate, 0)

    def finish_spread():
        cross.wait_send()
        for f, way in both:
            line_copy(f, way).wait_send()
            hop_copy(f, way).wait_send()
        for j in range(SPAN):
            for f, way in both:
                row_copy(f, j, way).wait_send()
                turn_copy(f, j, way).wait_send()

        def done(j, carry):
            mate_copy(j, core).wait_send()
            return carry

        lax.fori_loop(0, chips, done, 0)

    def mate_wait(j, carry):
        mate_copy(j, 1 - core).wait_recv()
        return carry

    def natural(k, tile):
        return pl.ds(pl.multiple_of(k * chunk * subs + tile * chunk, chunk), chunk)

    def near_gates(k):
        at = pl.ds(mul(k, chunk), chunk)

        def tile_step(n, inner):
            cols = pl.ds(mul(n, size), size)
            for gate, target in ((0, sbuf), (1, obuf)):
                total = jnp.dot(x[0, at, :], w[0, gate, :, cols], preferred_element_type=F32)
                total += jnp.dot(x[1, at, :], w[1, gate, :, cols], preferred_element_type=F32)
                total += jnp.dot(x[2, at, :], w[2, gate, :, cols], preferred_element_type=F32)
                for p in range(size // LANES):
                    target[natural(k, n * (size // LANES) + p), :] = total[:, p * LANES : (p + 1) * LANES]
            return inner

        lax.fori_loop(0, tiles, tile_step, 0)

    x_copy.wait()
    for slot in range(4):
        w_copy(slot).wait()
    begin_lines()
    for k in range(CHUNKS):
        pass_on(k)
        if k == 0:
            begin_hops()
        elif k == 1:
            begin_last_row()
            turn(0)
        elif k == 2:
            turn(1)
            turn(3)
        else:
            turn(2)
        near_gates(k)

    gain = gain_ref[...]
    start = start_ref[...]
    first_prev = jnp.where(me == 0, start, jnp.zeros_like(start))

    def far_gates(k):
        await_far(k)
        at = pl.ds(mul(k, chunk), chunk)

        def tile_step(n, inner):
            cols = pl.ds(mul(n, size), size)
            for gate, base, bias, target in ((0, sbuf, bias_u, ubuf), (1, obuf, bias_c, cbuf)):
                total = jnp.dot(x[3, at, :], w[3, gate, :, cols], preferred_element_type=F32)
                for p in range(size // LANES):
                    tile = n * (size // LANES) + p
                    part = total[:, p * LANES : (p + 1) * LANES] + base[natural(k, tile), :]
                    part = part + bias[:, pl.ds(mul(tile, LANES), LANES)]
                    part = part.astype(BF16).astype(F32)
                    if gate == 0:
                        part = 1.0 / (1.0 + jnp.exp(-part))
                    target[pl.ds(k * chunk * subs + tile, chunk, stride=subs), :] = part
            return inner

        lax.fori_loop(0, tiles, tile_step, 0)

    def token(ref, t):
        return ref[pl.ds(mul(t, subs), subs), :]

    def put(ref, t, value):
        ref[pl.ds(mul(t, subs), subs), :] = value

    def first_block(b, carry):
        acc_s, acc_o = carry
        base = b * BLOCK
        lead = jnp.where(b == 0, first_prev, jnp.zeros_like(start))
        for i in range(BLOCK):
            update = token(ubuf, base + i)
            cand = token(cbuf, base + i)
            keep = 1.0 - update
            if i == 0:
                squashed = jnp.tanh(cand + gain * lead)
                slope = keep + update * gain * (1.0 - squashed * squashed)
                offset = keep * lead + update * squashed - slope * lead
            else:
                squashed = jnp.tanh(cand)
                slope = keep + update * gain * (1.0 - squashed * squashed)
                offset = update * squashed
            put(sbuf, base + i, slope)
            put(obuf, base + i, offset)
            acc_o = slope * acc_o + offset
            acc_s = slope * acc_s
        return acc_s, acc_o

    blocks = chunk // BLOCK

    def far_step(k, carry):
        far_gates(k)
        return lax.fori_loop(k * blocks, (k + 1) * blocks, first_block, carry)

    ident = (jnp.ones_like(start), jnp.zeros_like(start))
    carry = lax.fori_loop(0, CHUNKS - 1, far_step, ident)
    begin_mates()
    carry = far_step(CHUNKS - 1, carry)

    def message(stage_no, source, target):
        return pltpu.make_async_remote_copy(
            src_ref=msg.at[stage_no],
            dst_ref=inbox.at[stage_no, source],
            send_sem=msg_send.at[target],
            recv_sem=msg_recv.at[stage_no, source],
            device_id={"ctx": target},
            device_id_type=pl.DeviceIdType.MESH,
        )

    def send_maps(stage_no, maps):
        msg[stage_no, pl.ds(0, subs), :] = maps[0]
        msg[stage_no, pl.ds(subs, subs), :] = maps[1]

        def post(d, c):
            message(stage_no, me, d).start()
            return c

        lax.fori_loop(me + 1, n_ctx, post, 0)

    def entering(stage_no):
        def take(d, h):
            message(stage_no, d, d).wait_recv()
            return inbox[stage_no, d, pl.ds(0, subs), :] * h + inbox[stage_no, d, pl.ds(subs, subs), :]

        return lax.fori_loop(0, me, take, start)

    def posted(stage_no):
        def done(d, c):
            message(stage_no, me, d).wait_send()
            return c

        lax.fori_loop(me + 1, n_ctx, done, 0)

    send_maps(0, carry)
    lax.fori_loop(0, CHUNKS, finish_sends, 0)
    for neighbour in (pair, across):
        pl.semaphore_signal(free, inc=1, device_id={"ch": neighbour}, device_id_type=pl.DeviceIdType.MESH)
    state = entering(0)
    posted(0)

    def second_block(b, carry):
        h, acc_s, acc_o = carry
        base = b * BLOCK
        for i in range(BLOCK):
            prev = h
            h = token(sbuf, base + i) * h + token(obuf, base + i)
            update = token(ubuf, base + i)
            cand = token(cbuf, base + i)
            keep = 1.0 - update
            squashed = jnp.tanh(cand + gain * prev)
            slope = keep + update * gain * (1.0 - squashed * squashed)
            offset = keep * prev + update * squashed - slope * prev
            put(sbuf, base + i, slope)
            put(obuf, base + i, offset)
            acc_o = slope * acc_o + offset
            acc_s = slope * acc_s
        return h, acc_s, acc_o

    final = lax.fori_loop(0, CHUNKS * blocks, second_block, (state,) + ident)
    send_maps(1, final[1:])
    state = entering(1)
    posted(1)
    pl.semaphore_wait(free, 2)

    def last_block(b, h):
        base = b * BLOCK
        for i in range(BLOCK):
            h = token(sbuf, base + i) * h + token(obuf, base + i)
            put(ubuf, base + i, h)
        return h

    def state_copy(k, goes_across):
        at = pl.ds(mul(2 * k + jnp.where(goes_across, mine, 1 - mine), part_rows), part_rows)
        slot = jnp.where(goes_across, 1, 0)
        return pltpu.make_async_remote_copy(
            src_ref=x.at[0, at, :],
            dst_ref=x.at[1 + slot, pl.ds(mul(k, part_rows), part_rows), :],
            send_sem=own_send.at[slot, k],
            recv_sem=own_recv.at[slot, k],
            device_id={"ch": jnp.where(goes_across, across, pair)},
            device_id_type=pl.DeviceIdType.MESH,
        )

    def state_fwd(k):
        at = pl.ds(mul(k, part_rows), part_rows)
        return pltpu.make_async_remote_copy(
            src_ref=x.at[1, at, :],
            dst_ref=x.at[3, at, :],
            send_sem=fwd_send.at[0, k],
            recv_sem=fwd_recv.at[0, k],
            device_id={"ch": across},
            device_id_type=pl.DeviceIdType.MESH,
        )

    part_blocks = part_rows // BLOCK

    def last_step(c, h):
        h = lax.fori_loop(c * part_blocks, (c + 1) * part_blocks, last_block, h)
        at = pl.ds(mul(c, part_rows), part_rows)
        for tile in range(subs):
            values = ubuf[pl.ds(c * part_rows * subs + tile, part_rows, stride=subs), :]
            x[0, at, tile * LANES : (tile + 1) * LANES] = values.astype(BF16)
        state_copy(lax.div(c, 2), lax.rem(c, 2) == mine).start()
        return h

    lax.fori_loop(0, 2 * CHUNKS, last_step, state)
    lax.fori_loop(0, chips, mate_wait, 0)

    def w_part(side, slot, cols):
        return wo[side, pl.ds(mul(sources[slot], width), width), cols]

    def held(k, side, tile):
        return pl.ds(pl.multiple_of(((k * 2 + side) * subs + tile) * part_rows, part_rows), part_rows)

    def near_out(k, carry):
        state_copy(k, False).wait_recv()
        state_fwd(k).start()
        state_copy(k, True).wait_recv()
        own = pl.ds(mul(2 * k + mine, part_rows), part_rows)
        at = pl.ds(mul(k, part_rows), part_rows)

        def tile_step(n, inner):
            cols = pl.ds(mul(n, size), size)
            for side in range(2):
                total = jnp.dot(x[0, own, :], w_part(side, 0, cols), preferred_element_type=F32)
                total += jnp.dot(x[1, at, :], w_part(side, 1, cols), preferred_element_type=F32)
                total += jnp.dot(x[2, at, :], w_part(side, 2, cols), preferred_element_type=F32)
                for p in range(size // LANES):
                    cbuf[held(k, side, n * (size // LANES) + p), :] = total[:, p * LANES : (p + 1) * LANES]
            return inner

        lax.fori_loop(0, tiles, tile_step, 0)
        return carry

    lax.fori_loop(0, CHUNKS, near_out, 0)

    def out_copy(k):
        at = pl.ds(mul(k, part_rows), part_rows)
        to = pl.ds(mul(2 * k + mine, part_rows), part_rows)
        return pltpu.make_async_copy(w.at[0, 0, at, :], out.at[to, :], out_sem.at[k])

    def give_copy(k, half_at):
        at = pl.ds(mul(k, part_rows), part_rows)
        to = pl.ds(mul(2 * k + half_at, part_rows), part_rows)
        return pltpu.make_async_remote_copy(
            src_ref=w.at[0, 1, at, :],
            dst_ref=out.at[to, :],
            send_sem=give_send.at[k],
            recv_sem=give_recv.at[k],
            device_id={"ch": pair},
            device_id_type=pl.DeviceIdType.MESH,
        )

    def far_out(k, carry):
        state_fwd(k).wait_recv()
        at = pl.ds(mul(k, part_rows), part_rows)
        for side in (1, 0):

            def tile_step(n, inner):
                cols = pl.ds(mul(n, size), size)
                total = jnp.dot(x[3, at, :], w_part(side, 3, cols), preferred_element_type=F32)
                for p in range(size // LANES):
                    tile = n * (size // LANES) + p
                    part = total[:, p * LANES : (p + 1) * LANES] + cbuf[held(k, side, tile), :]
                    w[0, side, at, pl.ds(mul(tile, LANES), LANES)] = part.astype(BF16)
                return inner

            lax.fori_loop(0, tiles, tile_step, 0)
            if side == 1:
                give_copy(k, mine).start()
            else:
                out_copy(k).start()
        return carry

    lax.fori_loop(0, CHUNKS, far_out, 0)
    finish_spread()

    def last_waits(k, carry):
        state_copy(k, False).wait_send()
        state_copy(k, True).wait_send()
        state_fwd(k).wait_send()
        out_copy(k).wait()
        give_copy(k, mine).wait_send()
        give_copy(k, 1 - mine).wait_recv()
        return carry

    lax.fori_loop(0, CHUNKS, last_waits, 0)


def on_device(tokens, w_input, w_output, bias_update, bias_cand, recur_gain, start_state):
    rows, width = tokens.shape
    subs = width // LANES
    n_ctx = lax.axis_size("ctx")
    n_ch = lax.axis_size("ch")
    any_spec = pl.BlockSpec(memory_space=pl.ANY)
    vmem_spec = pl.BlockSpec(memory_space=pltpu.VMEM)
    dma = pltpu.SemaphoreType.DMA
    return pl.pallas_call(
        functools.partial(kernel, n_ctx, n_ch, rows, width),
        out_shape=jax.ShapeDtypeStruct((rows, width), BF16),
        in_specs=[any_spec] * 3 + [vmem_spec] * 4,
        out_specs=any_spec,
        scratch_shapes=[
            pltpu.VMEM((4, rows, width), BF16),
            pltpu.VMEM((4, 2, width, width), BF16),
            pltpu.VMEM((2, n_ch * width, width), BF16),
            pltpu.VMEM((rows * subs, LANES), F32),
            pltpu.VMEM((rows * subs, LANES), F32),
            pltpu.VMEM((rows * subs, LANES), F32),
            pltpu.VMEM((rows * subs, LANES), F32),
            pltpu.VMEM((2, 2 * subs, LANES), F32),
            pltpu.VMEM((2, n_ctx, 2 * subs, LANES), F32),
            dma((2, CHUNKS)),
            dma((2, CHUNKS)),
            dma((2, CHUNKS)),
            dma((2, CHUNKS)),
            dma((2, 2)),
            dma((2, 2)),
            dma((2, 2)),
            dma((2, 2)),
            dma((2, SPAN, 2)),
            dma((2, SPAN, 2)),
            dma((2, SPAN, 2)),
            dma((2, SPAN, 2)),
            dma((n_ctx // 2,)),
            dma((n_ctx // 2,)),
            dma((CHUNKS,)),
            dma((CHUNKS,)),
            dma,
            dma,
            dma,
            dma((4,)),
            dma,
            dma((CHUNKS,)),
            dma((n_ctx,)),
            dma((2, n_ctx)),
            pltpu.SemaphoreType.REGULAR,
        ],
        compiler_params=pltpu.CompilerParams(
            collective_id=0, has_side_effects=True, vmem_limit_bytes=61 * 1024 * 1024
        ),
        cost_estimate=pl.CostEstimate(
            flops=6 * rows * width * width * n_ch,
            bytes_accessed=2 * (2 * rows * width + 3 * width * width * n_ch),
            transcendentals=4 * rows * width,
        ),
    )(
        tokens,
        w_input,
        w_output,
        bias_update.reshape(1, width),
        bias_cand.reshape(1, width),
        recur_gain.reshape(subs, LANES),
        start_state.reshape(subs, LANES),
    )


def solution(mesh):
    return jax.shard_map(
        on_device,
        mesh=mesh,
        in_specs=(
            P("ctx", "ch"),
            P(None, None, "ch"),
            P("ctx", "ch"),
            P("ch"),
            P("ch"),
            P("ch"),
            P("ch"),
        ),
        out_specs=P("ctx", "ch"),
        check_vma=False,
    )
```

```python
import functools

import jax
import jax.numpy as jnp
from jax import lax
from jax.experimental import pallas as pl
from jax.experimental.pallas import tpu as pltpu
from jax.sharding import PartitionSpec as P

LANES = 128
CHUNKS = 4
FINE = 16
TILE = 256
BLOCK = 16
SPAN = 4
F32 = jnp.float32
BF16 = jnp.bfloat16


def mul(index, size):
    return pl.multiple_of(index * size, size)


def kernel(
    n_ctx, n_ch, rows, width,
    tok, w_in, w_out, bias_u, bias_c, gain_ref, start_ref, out,
    x, w, wo, ubuf, cbuf, sbuf, obuf, msg, inbox,
    own_send, own_recv, fwd_send, fwd_recv,
    line_send, line_recv, hop_send, hop_recv,
    row_send, row_recv, turn_send, turn_recv,
    mate_send, mate_recv, give_send, give_recv, cross_send, cross_recv,
    x_sem, w_sem, wo_sem, out_sem, msg_send, msg_recv, free,
):
    subs = width // LANES
    size = min(TILE, width)
    me = lax.axis_index("ctx")
    col = lax.axis_index("ch")
    pair = col + 1 - 2 * lax.rem(col, 2)
    across = n_ch - 1 - col
    far = lax.rem(col + 2, n_ch)
    sources = (col, pair, across, far)
    mine = lax.rem(lax.div(col + 1, 2), 2)
    chunk = rows // CHUNKS
    fine = rows // FINE
    pieces = [(k * chunk, chunk, chunk * 7 // 16) for k in range(CHUNKS - 1)]
    pieces += [(rows - chunk, chunk // 2, chunk // 4), (rows - chunk // 2, chunk // 2, chunk * 3 // 16)]
    wo_rows = w_out.shape[0]
    chips = n_ctx // 2
    core = lax.rem(me, 2)
    mate = me + 1 - 2 * core
    tiles = width // size
    y_at = lax.div(me, 2 * SPAN)
    z_at = lax.rem(lax.div(me, 2), SPAN)

    def spot(f, first, second):
        first = lax.rem(first + SPAN, SPAN)
        second = lax.rem(second + SPAN, SPAN)
        y, z = (first, second) if f == 0 else (second, first)
        return (y * SPAN + z) * 2 + core

    barrier = pltpu.get_barrier_semaphore()
    for neighbour in (pair, across):
        pl.semaphore_signal(barrier, inc=1, device_id={"ch": neighbour}, device_id_type=pl.DeviceIdType.MESH)
    around = [spot(0, y_at + 1, z_at), spot(0, y_at - 1, z_at), spot(0, y_at, z_at + 1), spot(0, y_at, z_at - 1), mate]
    for neighbour in around:
        pl.semaphore_signal(barrier, inc=1, device_id={"ctx": neighbour}, device_id_type=pl.DeviceIdType.MESH)
    pl.semaphore_wait(barrier, 2 + len(around))

    def wo_piece(owner, low, count):
        return wo.at[:, pl.ds(pl.multiple_of(owner * wo_rows + low, 16), count), :]

    wo_copy = pltpu.make_async_copy(w_out, wo.at[0, pl.ds(mul(me, wo_rows), wo_rows), :], wo_sem)
    wo_copy.start()
    cross = pltpu.make_async_remote_copy(
        src_ref=w_out,
        dst_ref=wo.at[1, pl.ds(mul(me, wo_rows), wo_rows), :],
        send_sem=cross_send,
        recv_sem=cross_recv,
        device_id={"ch": pair},
        device_id_type=pl.DeviceIdType.MESH,
    )
    cross.start()

    def own_copy(source, way, k):
        low, count, _ = pieces[k]
        peer = (pair, across)[way]
        return pltpu.make_async_remote_copy(
            src_ref=source.at[pl.ds(low, count), :],
            dst_ref=x.at[1 + way, pl.ds(low, count), :],
            send_sem=own_send.at[way, k],
            recv_sem=own_recv.at[way, k],
            device_id={"ch": peer},
            device_id_type=pl.DeviceIdType.MESH,
        )

    def fwd_copy(way, k):
        low, count, share = pieces[k]
        peer = (across, pair)[way]
        at = pl.ds(low, count - share) if way == 0 else pl.ds(low + count - share, share)
        return pltpu.make_async_remote_copy(
            src_ref=x.at[1 + way, at, :],
            dst_ref=x.at[3, at, :],
            send_sem=fwd_send.at[way, k],
            recv_sem=fwd_recv.at[way, k],
            device_id={"ch": peer},
            device_id_type=pl.DeviceIdType.MESH,
        )

    def pass_on(k):
        for way in range(2):
            own_copy(tok, way, k).wait_recv()
            fwd_copy(way, k).start()

    def await_far(k):
        for way in range(2):
            fwd_copy(way, k).wait_recv()

    for k in range(len(pieces)):
        for way in range(2):
            own_copy(tok, way, k).start()

    x_copy = pltpu.make_async_copy(tok, x.at[0], x_sem)
    x_copy.start()

    def w_copy(slot):
        return pltpu.make_async_copy(
            w_in.at[:, pl.ds(mul(sources[slot], width), width), :], w.at[slot], w_sem.at[slot]
        )

    for slot in range(4):
        w_copy(slot).start()

    half = wo_rows // 2
    quarter = half // 2

    def line_copy(f, way):
        a, b = (y_at, z_at) if f == 0 else (z_at, y_at)
        step = 1 - 2 * way
        piece = wo_piece(me, f * half, half)
        return pltpu.make_async_remote_copy(
            src_ref=piece, dst_ref=piece,
            send_sem=line_send.at[f, way], recv_sem=line_recv.at[f, way],
            device_id={"ctx": spot(f, a + step, b)}, device_id_type=pl.DeviceIdType.MESH,
        )

    def hop_copy(f, way):
        a, b = (y_at, z_at) if f == 0 else (z_at, y_at)
        step = 1 - 2 * way
        piece = wo_piece(spot(f, a - step, b), f * half + way * quarter, quarter)
        return pltpu.make_async_remote_copy(
            src_ref=piece, dst_ref=piece,
            send_sem=hop_send.at[f, way], recv_sem=hop_recv.at[f, way],
            device_id={"ctx": spot(f, a + step, b)}, device_id_type=pl.DeviceIdType.MESH,
        )

    def row_copy(f, j, way):
        a, b = (y_at, z_at) if f == 0 else (z_at, y_at)
        step = 1 - 2 * way
        piece = wo_piece(spot(f, a + j, b), f * half, half)
        return pltpu.make_async_remote_copy(
            src_ref=piece, dst_ref=piece,
            send_sem=row_send.at[f, j, way], recv_sem=row_recv.at[f, j, way],
            device_id={"ctx": spot(f, a, b + step)}, device_id_type=pl.DeviceIdType.MESH,
        )

    def turn_copy(f, j, way):
        a, b = (y_at, z_at) if f == 0 else (z_at, y_at)
        step = 1 - 2 * way
        piece = wo_piece(spot(f, a + j, b - step), f * half + way * quarter, quarter)
        return pltpu.make_async_remote_copy(
            src_ref=piece, dst_ref=piece,
            send_sem=turn_send.at[f, j, way], recv_sem=turn_recv.at[f, j, way],
            device_id={"ctx": spot(f, a, b + step)}, device_id_type=pl.DeviceIdType.MESH,
        )

    def mate_copy(f, owner):
        piece = wo_piece(owner, f * half, half)
        return pltpu.make_async_remote_copy(
            src_ref=piece, dst_ref=piece,
            send_sem=mate_send.at[f, lax.div(owner, 2)], recv_sem=mate_recv.at[f, lax.div(owner, 2)],
            device_id={"ctx": mate}, device_id_type=pl.DeviceIdType.MESH,
        )

    def share(f, first, second):
        a, b = (y_at, z_at) if f == 0 else (z_at, y_at)
        mate_copy(f, spot(f, a + first, b + second)).start()

    both = [(f, way) for f in range(2) for way in range(2)]

    def begin_lines():
        wo_copy.wait()
        cross.wait_recv()
        for f, way in both:
            line_copy(f, way).start()
        for f, way in both:
            row_copy(f, 0, way).start()
        for f in range(2):
            share(f, 0, 0)

    def begin_hops():
        for f, way in both:
            line_copy(f, way).wait_recv()
            hop_copy(f, way).start()
        for j in (1, 3):
            for f, way in both:
                row_copy(f, j, way).start()
        for j in (1, 3):
            for f in range(2):
                share(f, j, 0)

    def begin_last_row():
        for f, way in both:
            hop_copy(f, way).wait_recv()
        for f, way in both:
            row_copy(f, 2, way).start()
        for f in range(2):
            share(f, 2, 0)

    def turn(j):
        for f, way in both:
            row_copy(f, j, way).wait_recv()
            turn_copy(f, j, way).start()
        for f, way in both:
            share(f, j, 2 * way - 1)

    def turned(j):
        for f, way in both:
            turn_copy(f, j, way).wait_recv()
        for f in range(2):
            share(f, j, 2)

    def finish_spread():
        cross.wait_send()
        for f, way in both:
            line_copy(f, way).wait_send()
            hop_copy(f, way).wait_send()
        for j in range(SPAN):
            for f, way in both:
                row_copy(f, j, way).wait_send()
                turn_copy(f, j, way).wait_send()

        def done(j, carry):
            for f in range(2):
                mate_copy(f, 2 * j + core).wait_send()
            return carry

        lax.fori_loop(0, chips, done, 0)

    def mate_wait(j, carry):
        for f in range(2):
            mate_copy(f, 2 * j + 1 - core).wait_recv()
        return carry

    def natural(k, tile):
        low, count, _ = pieces[k]
        return pl.ds(pl.multiple_of(low * subs + tile * count, count), count)

    def near_gates(k):
        at = pl.ds(pieces[k][0], pieces[k][1])

        def tile_step(n, inner):
            cols = pl.ds(mul(n, size), size)
            for gate, target in ((0, sbuf), (1, obuf)):
                total = jnp.dot(x[0, at, :], w[0, gate, :, cols], preferred_element_type=F32)
                total += jnp.dot(x[1, at, :], w[1, gate, :, cols], preferred_element_type=F32)
                total += jnp.dot(x[2, at, :], w[2, gate, :, cols], preferred_element_type=F32)
                for p in range(size // LANES):
                    target[natural(k, n * (size // LANES) + p), :] = total[:, p * LANES : (p + 1) * LANES]
            return inner

        lax.fori_loop(0, tiles, tile_step, 0)

    x_copy.wait()
    for slot in range(4):
        w_copy(slot).wait()
    begin_lines()
    for k in range(len(pieces)):
        pass_on(k)
        if k == 0:
            begin_hops()
        elif k == 1:
            begin_last_row()
            turn(0)
        elif k == 2:
            turn(1)
            turn(3)
        elif k == 3:
            turn(2)
        near_gates(k)

    gain = gain_ref[...]
    start = start_ref[...]
    first_prev = jnp.where(me == 0, start, jnp.zeros_like(start))

    def far_gates(k):
        await_far(k)
        low, count, _ = pieces[k]
        at = pl.ds(low, count)

        def tile_step(n, inner):
            cols = pl.ds(mul(n, size), size)
            for gate, base, bias, target in ((0, sbuf, bias_u, ubuf), (1, obuf, bias_c, cbuf)):
                total = jnp.dot(x[3, at, :], w[3, gate, :, cols], preferred_element_type=F32)
                for p in range(size // LANES):
                    tile = n * (size // LANES) + p
                    part = total[:, p * LANES : (p + 1) * LANES] + base[natural(k, tile), :]
                    part = part + bias[:, pl.ds(mul(tile, LANES), LANES)]
                    part = part.astype(BF16).astype(F32)
                    if gate == 0:
                        part = 1.0 / (1.0 + jnp.exp(-part))
                    target[pl.ds(low * subs + tile, count, stride=subs), :] = part
            return inner

        lax.fori_loop(0, tiles, tile_step, 0)

    def token(ref, t):
        return ref[pl.ds(mul(t, subs), subs), :]

    def put(ref, t, value):
        ref[pl.ds(mul(t, subs), subs), :] = value

    def first_block(b, carry):
        acc_s, acc_o = carry
        base = b * BLOCK
        lead = jnp.where(b == 0, first_prev, jnp.zeros_like(start))
        for i in range(BLOCK):
            update = token(ubuf, base + i)
            cand = token(cbuf, base + i)
            keep = 1.0 - update
            if i == 0:
                squashed = jnp.tanh(cand + gain * lead)
                slope = keep + update * gain * (1.0 - squashed * squashed)
                offset = keep * lead + update * squashed - slope * lead
            else:
                squashed = jnp.tanh(cand)
                slope = keep + update * gain * (1.0 - squashed * squashed)
                offset = update * squashed
            put(sbuf, base + i, slope)
            put(obuf, base + i, offset)
            acc_o = slope * acc_o + offset
            acc_s = slope * acc_s
        return acc_s, acc_o

    def far_step(k, carry):
        far_gates(k)
        low, count, _ = pieces[k]
        return lax.fori_loop(low // BLOCK, (low + count) // BLOCK, first_block, carry)

    ident = (jnp.ones_like(start), jnp.zeros_like(start))
    carry = ident
    for k in range(len(pieces)):
        carry = far_step(k, carry)
        if k < 2:
            turned((0, 1)[k])
            turned((3, 2)[k])

    def message(stage_no, source, target):
        return pltpu.make_async_remote_copy(
            src_ref=msg.at[stage_no],
            dst_ref=inbox.at[stage_no, source],
            send_sem=msg_send.at[stage_no, target],
            recv_sem=msg_recv.at[stage_no, source],
            device_id={"ctx": target},
            device_id_type=pl.DeviceIdType.MESH,
        )

    def send_maps(stage_no, maps):
        msg[stage_no, pl.ds(0, subs), :] = maps[0]
        msg[stage_no, pl.ds(subs, subs), :] = maps[1]

        def post(d, c):
            message(stage_no, me, d).start()
            return c

        lax.fori_loop(me + 1, n_ctx, post, 0)

    def entering(stage_no):
        def take(d, h):
            message(stage_no, d, d).wait_recv()
            return inbox[stage_no, d, pl.ds(0, subs), :] * h + inbox[stage_no, d, pl.ds(subs, subs), :]

        return lax.fori_loop(0, me, take, start)

    def posted(stage_no):
        def done(d, c):
            message(stage_no, me, d).wait_send()
            return c

        lax.fori_loop(me + 1, n_ctx, done, 0)

    send_maps(0, carry)
    for k in range(len(pieces)):
        for way in range(2):
            own_copy(tok, way, k).wait_send()
            fwd_copy(way, k).wait_send()
    for neighbour in (pair, across):
        pl.semaphore_signal(free, inc=1, device_id={"ch": neighbour}, device_id_type=pl.DeviceIdType.MESH)
    state = entering(0)

    def second_block(b, carry):
        h, acc_s, acc_o = carry
        base = b * BLOCK
        for i in range(BLOCK):
            prev = h
            h = token(sbuf, base + i) * h + token(obuf, base + i)
            update = token(ubuf, base + i)
            cand = token(cbuf, base + i)
            keep = 1.0 - update
            squashed = jnp.tanh(cand + gain * prev)
            slope = keep + update * gain * (1.0 - squashed * squashed)
            offset = keep * prev + update * squashed - slope * prev
            put(sbuf, base + i, slope)
            put(obuf, base + i, offset)
            acc_o = slope * acc_o + offset
            acc_s = slope * acc_s
        return h, acc_s, acc_o

    final = lax.fori_loop(0, rows // BLOCK, second_block, (state,) + ident)
    send_maps(1, final[1:])
    state = entering(1)
    pl.semaphore_wait(free, 2)

    def last_block(b, h):
        base = b * BLOCK
        for i in range(BLOCK):
            h = token(sbuf, base + i) * h + token(obuf, base + i)
            put(ubuf, base + i, h)
        return h

    def sides(k, which):
        return pl.ds(pl.multiple_of(which * (rows // 2) + k * fine, fine), fine)

    def state_copy(k, goes_across):
        slot = jnp.where(goes_across, 1, 0)
        return pltpu.make_async_remote_copy(
            src_ref=x.at[0, sides(k, jnp.where(goes_across, mine, 1 - mine)), :],
            dst_ref=x.at[1 + slot, pl.ds(mul(k, fine), fine), :],
            send_sem=own_send.at[slot, k],
            recv_sem=own_recv.at[slot, k],
            device_id={"ch": jnp.where(goes_across, across, pair)},
            device_id_type=pl.DeviceIdType.MESH,
        )

    def state_fwd(k):
        at = pl.ds(mul(k, fine), fine)
        return pltpu.make_async_remote_copy(
            src_ref=x.at[1, at, :],
            dst_ref=x.at[3, at, :],
            send_sem=fwd_send.at[0, k],
            recv_sem=fwd_recv.at[0, k],
            device_id={"ch": across},
            device_id_type=pl.DeviceIdType.MESH,
        )

    def last_step(c, h):
        h = lax.fori_loop(c * (fine // BLOCK), (c + 1) * (fine // BLOCK), last_block, h)
        at = sides(lax.div(c, 2), lax.rem(c, 2))
        for tile in range(subs):
            values = ubuf[pl.ds(c * fine * subs + tile, fine, stride=subs), :]
            x[0, at, tile * LANES : (tile + 1) * LANES] = values.astype(BF16)
        state_copy(lax.div(c, 2), lax.rem(c, 2) == mine).start()
        return h

    lax.fori_loop(0, FINE, last_step, state)
    lax.fori_loop(0, chips, mate_wait, 0)

    def w_part(side, slot, cols):
        return wo[side, pl.ds(mul(sources[slot], width), width), cols]

    def held(k, side, tile):
        return pl.ds(pl.multiple_of(((k * 2 + side) * subs + tile) * 2 * fine, 2 * fine), 2 * fine)

    def held_half(k, side, tile):
        low = ((lax.div(k, 2) * 2 + side) * subs + tile) * 2 * fine + lax.rem(k, 2) * fine
        return pl.ds(pl.multiple_of(low, fine), fine)

    def near_out(k, carry):
        for e in range(2):
            state_copy(2 * k + e, False).wait_recv()
            state_fwd(2 * k + e).start()
        for e in range(2):
            state_copy(2 * k + e, True).wait_recv()
        own = pl.ds(pl.multiple_of(mine * (rows // 2) + k * 2 * fine, 2 * fine), 2 * fine)
        at = pl.ds(mul(k, 2 * fine), 2 * fine)

        def tile_step(n, inner):
            cols = pl.ds(mul(n, size), size)
            for side in range(2):
                total = jnp.dot(x[0, own, :], w_part(side, 0, cols), preferred_element_type=F32)
                total += jnp.dot(x[1, at, :], w_part(side, 1, cols), preferred_element_type=F32)
                total += jnp.dot(x[2, at, :], w_part(side, 2, cols), preferred_element_type=F32)
                for p in range(size // LANES):
                    cbuf[held(k, side, n * (size // LANES) + p), :] = total[:, p * LANES : (p + 1) * LANES]
            return inner

        lax.fori_loop(0, tiles, tile_step, 0)
        return carry

    lax.fori_loop(0, FINE // 4, near_out, 0)

    def out_copy(k):
        at = pl.ds(mul(k, fine), fine)
        to = pl.ds(mul(2 * k + mine, fine), fine)
        return pltpu.make_async_copy(w.at[0, 0, at, :], out.at[to, :], out_sem.at[k])

    def give_copy(k, half_at):
        at = pl.ds(mul(k, fine), fine)
        to = pl.ds(mul(2 * k + half_at, fine), fine)
        return pltpu.make_async_remote_copy(
            src_ref=w.at[0, 1, at, :],
            dst_ref=out.at[to, :],
            send_sem=give_send.at[k],
            recv_sem=give_recv.at[k],
            device_id={"ch": pair},
            device_id_type=pl.DeviceIdType.MESH,
        )

    def far_out(k, carry):
        state_fwd(k).wait_recv()
        at = pl.ds(mul(k, fine), fine)
        for side in (1, 0):

            def tile_step(n, inner):
                cols = pl.ds(mul(n, size), size)
                total = jnp.dot(x[3, at, :], w_part(side, 3, cols), preferred_element_type=F32)
                for p in range(size // LANES):
                    tile = n * (size // LANES) + p
                    part = total[:, p * LANES : (p + 1) * LANES] + cbuf[held_half(k, side, tile), :]
                    w[0, side, at, pl.ds(mul(tile, LANES), LANES)] = part.astype(BF16)
                return inner

            lax.fori_loop(0, tiles, tile_step, 0)
            if side == 1:
                give_copy(k, mine).start()
            else:
                out_copy(k).start()
        return carry

    lax.fori_loop(0, FINE // 2, far_out, 0)
    finish_spread()
    posted(0)
    posted(1)

    def last_waits(k, carry):
        state_copy(k, False).wait_send()
        state_copy(k, True).wait_send()
        state_fwd(k).wait_send()
        out_copy(k).wait()
        give_copy(k, mine).wait_send()
        give_copy(k, 1 - mine).wait_recv()
        return carry

    lax.fori_loop(0, FINE // 2, last_waits, 0)


def on_device(tokens, w_input, w_output, bias_update, bias_cand, recur_gain, start_state):
    rows, width = tokens.shape
    subs = width // LANES
    n_ctx = lax.axis_size("ctx")
    n_ch = lax.axis_size("ch")
    any_spec = pl.BlockSpec(memory_space=pl.ANY)
    vmem_spec = pl.BlockSpec(memory_space=pltpu.VMEM)
    dma = pltpu.SemaphoreType.DMA
    return pl.pallas_call(
        functools.partial(kernel, n_ctx, n_ch, rows, width),
        out_shape=jax.ShapeDtypeStruct((rows, width), BF16),
        in_specs=[any_spec] * 3 + [vmem_spec] * 4,
        out_specs=any_spec,
        scratch_shapes=[
            pltpu.VMEM((4, rows, width), BF16),
            pltpu.VMEM((4, 2, width, width), BF16),
            pltpu.VMEM((2, n_ch * width, width), BF16),
            pltpu.VMEM((rows * subs, LANES), F32),
            pltpu.VMEM((rows * subs, LANES), F32),
            pltpu.VMEM((rows * subs, LANES), F32),
            pltpu.VMEM((rows * subs, LANES), F32),
            pltpu.VMEM((2, 2 * subs, LANES), F32),
            pltpu.VMEM((2, n_ctx, 2 * subs, LANES), F32),
            dma((2, FINE // 2)),
            dma((2, FINE // 2)),
            dma((2, FINE // 2)),
            dma((2, FINE // 2)),
            dma((2, 2)),
            dma((2, 2)),
            dma((2, 2)),
            dma((2, 2)),
            dma((2, SPAN, 2)),
            dma((2, SPAN, 2)),
            dma((2, SPAN, 2)),
            dma((2, SPAN, 2)),
            dma((2, n_ctx // 2)),
            dma((2, n_ctx // 2)),
            dma((FINE // 2,)),
            dma((FINE // 2,)),
            dma,
            dma,
            dma,
            dma((4,)),
            dma,
            dma((FINE // 2,)),
            dma((2, n_ctx)),
            dma((2, n_ctx)),
            pltpu.SemaphoreType.REGULAR,
        ],
        compiler_params=pltpu.CompilerParams(
            collective_id=0, has_side_effects=True, vmem_limit_bytes=61 * 1024 * 1024
        ),
        cost_estimate=pl.CostEstimate(
            flops=6 * rows * width * width * n_ch,
            bytes_accessed=2 * (2 * rows * width + 3 * width * width * n_ch),
            transcendentals=4 * rows * width,
        ),
    )(
        tokens,
        w_input,
        w_output,
        bias_update.reshape(1, width),
        bias_cand.reshape(1, width),
        recur_gain.reshape(subs, LANES),
        start_state.reshape(subs, LANES),
    )


def solution(mesh):
    return jax.shard_map(
        on_device,
        mesh=mesh,
        in_specs=(
            P("ctx", "ch"),
            P(None, None, "ch"),
            P("ctx", "ch"),
            P("ch"),
            P("ch"),
            P("ch"),
            P("ch"),
        ),
        out_specs=P("ctx", "ch"),
        check_vma=False,
    )
```

```python
import functools

import jax
import jax.numpy as jnp
from jax import lax
from jax.experimental import pallas as pl
from jax.experimental.pallas import tpu as pltpu
from jax.sharding import PartitionSpec as P

LANES = 128
CHUNKS = 4
FINE = 16
PIECES = 8
TILE = 256
BLOCK = 16
SPAN = 4
F32 = jnp.float32
BF16 = jnp.bfloat16


def mul(index, size):
    return pl.multiple_of(index * size, size)


def kernel(
    n_ctx, n_ch, rows, width,
    tok, w_in, w_out, bias_u, bias_c, gain_ref, start_ref, out,
    x, w, wo, ubuf, cbuf, sbuf, obuf, msg, inbox,
    own_send, own_recv, fwd_send, fwd_recv,
    line_send, line_recv, hop_send, hop_recv,
    row_send, row_recv, turn_send, turn_recv,
    mate_send, mate_recv, give_send, give_recv, cross_send, cross_recv,
    x_sem, w_sem, wo_sem, out_sem, msg_send, msg_recv, free,
):
    subs = width // LANES
    size = min(TILE, width)
    me = lax.axis_index("ctx")
    col = lax.axis_index("ch")
    pair = col + 1 - 2 * lax.rem(col, 2)
    across = n_ch - 1 - col
    far = lax.rem(col + 2, n_ch)
    sources = (col, pair, across, far)
    mine = lax.rem(lax.div(col + 1, 2), 2)
    chunk = rows // CHUNKS
    fine = rows // FINE
    pieces = [(k * chunk, chunk, chunk * 7 // 16) for k in range(CHUNKS - 1)]
    pieces += [(rows - chunk, chunk // 2, chunk // 4), (rows - chunk // 2, chunk // 2, chunk * 3 // 16)]
    wo_rows = w_out.shape[0]
    chips = n_ctx // 2
    core = lax.rem(me, 2)
    mate = me + 1 - 2 * core
    tiles = width // size
    y_at = lax.div(me, 2 * SPAN)
    z_at = lax.rem(lax.div(me, 2), SPAN)

    def spot(f, first, second):
        first = lax.rem(first + SPAN, SPAN)
        second = lax.rem(second + SPAN, SPAN)
        y, z = (first, second) if f == 0 else (second, first)
        return (y * SPAN + z) * 2 + core

    barrier = pltpu.get_barrier_semaphore()
    for neighbour in (pair, across):
        pl.semaphore_signal(barrier, inc=1, device_id={"ch": neighbour}, device_id_type=pl.DeviceIdType.MESH)
    around = [spot(0, y_at + 1, z_at), spot(0, y_at - 1, z_at), spot(0, y_at, z_at + 1), spot(0, y_at, z_at - 1), mate]
    for neighbour in around:
        pl.semaphore_signal(barrier, inc=1, device_id={"ctx": neighbour}, device_id_type=pl.DeviceIdType.MESH)
    pl.semaphore_wait(barrier, 2 + len(around))

    def wo_piece(owner, low, count):
        return wo.at[:, pl.ds(pl.multiple_of(owner * wo_rows + low, 16), count), :]

    wo_copy = pltpu.make_async_copy(w_out, wo.at[0, pl.ds(mul(me, wo_rows), wo_rows), :], wo_sem)
    wo_copy.start()
    cross = pltpu.make_async_remote_copy(
        src_ref=w_out,
        dst_ref=wo.at[1, pl.ds(mul(me, wo_rows), wo_rows), :],
        send_sem=cross_send,
        recv_sem=cross_recv,
        device_id={"ch": pair},
        device_id_type=pl.DeviceIdType.MESH,
    )
    cross.start()

    def own_copy(source, way, k):
        low, count, _ = pieces[k]
        peer = (pair, across)[way]
        return pltpu.make_async_remote_copy(
            src_ref=source.at[pl.ds(low, count), :],
            dst_ref=x.at[1 + way, pl.ds(low, count), :],
            send_sem=own_send.at[way, k],
            recv_sem=own_recv.at[way, k],
            device_id={"ch": peer},
            device_id_type=pl.DeviceIdType.MESH,
        )

    def fwd_copy(way, k):
        low, count, share = pieces[k]
        peer = (across, pair)[way]
        at = pl.ds(low, count - share) if way == 0 else pl.ds(low + count - share, share)
        return pltpu.make_async_remote_copy(
            src_ref=x.at[1 + way, at, :],
            dst_ref=x.at[3, at, :],
            send_sem=fwd_send.at[way, k],
            recv_sem=fwd_recv.at[way, k],
            device_id={"ch": peer},
            device_id_type=pl.DeviceIdType.MESH,
        )

    def pass_on(k):
        for way in range(2):
            own_copy(tok, way, k).wait_recv()
            fwd_copy(way, k).start()

    def await_far(k):
        for way in range(2):
            fwd_copy(way, k).wait_recv()

    for k in range(len(pieces)):
        for way in range(2):
            own_copy(tok, way, k).start()

    x_copy = pltpu.make_async_copy(tok, x.at[0], x_sem)
    x_copy.start()

    def w_copy(slot):
        return pltpu.make_async_copy(
            w_in.at[:, pl.ds(mul(sources[slot], width), width), :], w.at[slot], w_sem.at[slot]
        )

    for slot in range(4):
        w_copy(slot).start()

    half = wo_rows // 2
    quarter = half // 2

    def line_copy(f, way):
        a, b = (y_at, z_at) if f == 0 else (z_at, y_at)
        step = 1 - 2 * way
        piece = wo_piece(me, f * half, half)
        return pltpu.make_async_remote_copy(
            src_ref=piece, dst_ref=piece,
            send_sem=line_send.at[f, way], recv_sem=line_recv.at[f, way],
            device_id={"ctx": spot(f, a + step, b)}, device_id_type=pl.DeviceIdType.MESH,
        )

    def hop_copy(f, way):
        a, b = (y_at, z_at) if f == 0 else (z_at, y_at)
        step = 1 - 2 * way
        piece = wo_piece(spot(f, a - step, b), f * half + way * quarter, quarter)
        return pltpu.make_async_remote_copy(
            src_ref=piece, dst_ref=piece,
            send_sem=hop_send.at[f, way], recv_sem=hop_recv.at[f, way],
            device_id={"ctx": spot(f, a + step, b)}, device_id_type=pl.DeviceIdType.MESH,
        )

    def row_copy(f, j, way):
        a, b = (y_at, z_at) if f == 0 else (z_at, y_at)
        step = 1 - 2 * way
        piece = wo_piece(spot(f, a + j, b), f * half, half)
        return pltpu.make_async_remote_copy(
            src_ref=piece, dst_ref=piece,
            send_sem=row_send.at[f, j, way], recv_sem=row_recv.at[f, j, way],
            device_id={"ctx": spot(f, a, b + step)}, device_id_type=pl.DeviceIdType.MESH,
        )

    def turn_copy(f, j, way):
        a, b = (y_at, z_at) if f == 0 else (z_at, y_at)
        step = 1 - 2 * way
        piece = wo_piece(spot(f, a + j, b - step), f * half + way * quarter, quarter)
        return pltpu.make_async_remote_copy(
            src_ref=piece, dst_ref=piece,
            send_sem=turn_send.at[f, j, way], recv_sem=turn_recv.at[f, j, way],
            device_id={"ctx": spot(f, a, b + step)}, device_id_type=pl.DeviceIdType.MESH,
        )

    def mate_copy(f, owner):
        piece = wo_piece(owner, f * half, half)
        return pltpu.make_async_remote_copy(
            src_ref=piece, dst_ref=piece,
            send_sem=mate_send.at[f, lax.div(owner, 2)], recv_sem=mate_recv.at[f, lax.div(owner, 2)],
            device_id={"ctx": mate}, device_id_type=pl.DeviceIdType.MESH,
        )

    def share(f, first, second):
        a, b = (y_at, z_at) if f == 0 else (z_at, y_at)
        mate_copy(f, spot(f, a + first, b + second)).start()

    both = [(f, way) for f in range(2) for way in range(2)]

    def begin_lines():
        wo_copy.wait()
        cross.wait_recv()
        for f, way in both:
            line_copy(f, way).start()
        for f, way in both:
            row_copy(f, 0, way).start()
        for f in range(2):
            share(f, 0, 0)

    def begin_hops():
        for f, way in both:
            line_copy(f, way).wait_recv()
            hop_copy(f, way).start()
        for j in (1, 3):
            for f, way in both:
                row_copy(f, j, way).start()
        for j in (1, 3):
            for f in range(2):
                share(f, j, 0)

    def begin_last_row():
        for f, way in both:
            hop_copy(f, way).wait_recv()
        for f, way in both:
            row_copy(f, 2, way).start()
        for f in range(2):
            share(f, 2, 0)

    def turn(j):
        for f, way in both:
            row_copy(f, j, way).wait_recv()
            turn_copy(f, j, way).start()
        for f, way in both:
            share(f, j, 2 * way - 1)

    def turned(j):
        for f, way in both:
            turn_copy(f, j, way).wait_recv()
        for f in range(2):
            share(f, j, 2)

    def finish_spread():
        cross.wait_send()
        for f, way in both:
            line_copy(f, way).wait_send()
            hop_copy(f, way).wait_send()
        for j in range(SPAN):
            for f, way in both:
                row_copy(f, j, way).wait_send()
                turn_copy(f, j, way).wait_send()

        def done(j, carry):
            for f in range(2):
                mate_copy(f, 2 * j + core).wait_send()
            return carry

        lax.fori_loop(0, chips, done, 0)

    def mate_wait(j, carry):
        for f in range(2):
            mate_copy(f, 2 * j + 1 - core).wait_recv()
        return carry

    def natural(k, tile):
        low, count, _ = pieces[k]
        return pl.ds(pl.multiple_of(low * subs + tile * count, count), count)

    def near_gates(k):
        at = pl.ds(pieces[k][0], pieces[k][1])

        def tile_step(n, inner):
            cols = pl.ds(mul(n, size), size)
            for gate, target in ((0, sbuf), (1, obuf)):
                total = jnp.dot(x[0, at, :], w[0, gate, :, cols], preferred_element_type=F32)
                total += jnp.dot(x[1, at, :], w[1, gate, :, cols], preferred_element_type=F32)
                total += jnp.dot(x[2, at, :], w[2, gate, :, cols], preferred_element_type=F32)
                for p in range(size // LANES):
                    target[natural(k, n * (size // LANES) + p), :] = total[:, p * LANES : (p + 1) * LANES]
            return inner

        lax.fori_loop(0, tiles, tile_step, 0)

    x_copy.wait()
    for slot in range(4):
        w_copy(slot).wait()
    begin_lines()
    for k in range(len(pieces)):
        pass_on(k)
        if k == 0:
            begin_hops()
        elif k == 1:
            begin_last_row()
            turn(0)
        elif k == 2:
            turn(1)
            turn(3)
        elif k == 3:
            turn(2)
        near_gates(k)

    gain = gain_ref[...]
    start = start_ref[...]
    first_prev = jnp.where(me == 0, start, jnp.zeros_like(start))

    def far_gates(k):
        await_far(k)
        low, count, _ = pieces[k]
        at = pl.ds(low, count)

        def tile_step(n, inner):
            cols = pl.ds(mul(n, size), size)
            for gate, base, bias, target in ((0, sbuf, bias_u, ubuf), (1, obuf, bias_c, cbuf)):
                total = jnp.dot(x[3, at, :], w[3, gate, :, cols], preferred_element_type=F32)
                for p in range(size // LANES):
                    tile = n * (size // LANES) + p
                    part = total[:, p * LANES : (p + 1) * LANES] + base[natural(k, tile), :]
                    part = part + bias[:, pl.ds(mul(tile, LANES), LANES)]
                    part = part.astype(BF16).astype(F32)
                    if gate == 0:
                        part = 1.0 / (1.0 + jnp.exp(-part))
                    target[pl.ds(low * subs + tile, count, stride=subs), :] = part
            return inner

        lax.fori_loop(0, tiles, tile_step, 0)

    def token(ref, t):
        return ref[pl.ds(mul(t, subs), subs), :]

    def put(ref, t, value):
        ref[pl.ds(mul(t, subs), subs), :] = value

    def first_block(b, carry):
        acc_s, acc_o = carry
        base = b * BLOCK
        lead = jnp.where(b == 0, first_prev, jnp.zeros_like(start))
        for i in range(BLOCK):
            update = token(ubuf, base + i)
            cand = token(cbuf, base + i)
            keep = 1.0 - update
            if i == 0:
                squashed = jnp.tanh(cand + gain * lead)
                slope = keep + update * gain * (1.0 - squashed * squashed)
                offset = keep * lead + update * squashed - slope * lead
            else:
                squashed = jnp.tanh(cand)
                slope = keep + update * gain * (1.0 - squashed * squashed)
                offset = update * squashed
            put(sbuf, base + i, slope)
            put(obuf, base + i, offset)
            acc_o = slope * acc_o + offset
            acc_s = slope * acc_s
        return acc_s, acc_o

    def far_step(k, carry):
        far_gates(k)
        low, count, _ = pieces[k]
        return lax.fori_loop(low // BLOCK, (low + count) // BLOCK, first_block, carry)

    ident = (jnp.ones_like(start), jnp.zeros_like(start))
    carry = ident
    for k in range(len(pieces)):
        carry = far_step(k, carry)
        if k < 2:
            turned((0, 1)[k])
            turned((3, 2)[k])

    def message(stage_no, source, target):
        return pltpu.make_async_remote_copy(
            src_ref=msg.at[stage_no],
            dst_ref=inbox.at[stage_no, source],
            send_sem=msg_send.at[stage_no, target],
            recv_sem=msg_recv.at[stage_no, source],
            device_id={"ctx": target},
            device_id_type=pl.DeviceIdType.MESH,
        )

    def send_maps(stage_no, maps):
        msg[stage_no, pl.ds(0, subs), :] = maps[0]
        msg[stage_no, pl.ds(subs, subs), :] = maps[1]

        def post(d, c):
            message(stage_no, me, d).start()
            return c

        lax.fori_loop(me + 1, n_ctx, post, 0)

    def entering(stage_no):
        def take(d, h):
            message(stage_no, d, d).wait_recv()
            return inbox[stage_no, d, pl.ds(0, subs), :] * h + inbox[stage_no, d, pl.ds(subs, subs), :]

        return lax.fori_loop(0, me, take, start)

    def posted(stage_no):
        def done(d, c):
            message(stage_no, me, d).wait_send()
            return c

        lax.fori_loop(me + 1, n_ctx, done, 0)

    send_maps(0, carry)
    for k in range(len(pieces)):
        for way in range(2):
            own_copy(tok, way, k).wait_send()
            fwd_copy(way, k).wait_send()
    for neighbour in (pair, across):
        pl.semaphore_signal(free, inc=1, device_id={"ch": neighbour}, device_id_type=pl.DeviceIdType.MESH)
    state = entering(0)

    def second_block(b, carry):
        h, acc_s, acc_o = carry
        base = b * BLOCK
        for i in range(BLOCK):
            prev = h
            h = token(sbuf, base + i) * h + token(obuf, base + i)
            update = token(ubuf, base + i)
            cand = token(cbuf, base + i)
            keep = 1.0 - update
            squashed = jnp.tanh(cand + gain * prev)
            bend = update * gain * (1.0 - squashed * squashed)
            slope = keep + bend
            offset = update * squashed - bend * prev
            put(sbuf, base + i, slope)
            put(obuf, base + i, offset)
            acc_o = slope * acc_o + offset
            acc_s = slope * acc_s
        return h, acc_s, acc_o

    final = lax.fori_loop(0, rows // BLOCK, second_block, (state,) + ident)
    send_maps(1, final[1:])
    state = entering(1)
    pl.semaphore_wait(free, 2)

    def last_block(b, h):
        base = b * BLOCK
        for i in range(BLOCK):
            h = token(sbuf, base + i) * h + token(obuf, base + i)
            put(ubuf, base + i, h)
        return h

    def sides(k, which):
        return pl.ds(pl.multiple_of(which * (rows // 2) + k * fine, fine), fine)

    def state_copy(k, goes_across):
        slot = jnp.where(goes_across, 1, 0)
        return pltpu.make_async_remote_copy(
            src_ref=x.at[0, sides(k, jnp.where(goes_across, mine, 1 - mine)), :],
            dst_ref=x.at[1 + slot, pl.ds(mul(k, fine), fine), :],
            send_sem=own_send.at[slot, k],
            recv_sem=own_recv.at[slot, k],
            device_id={"ch": jnp.where(goes_across, across, pair)},
            device_id_type=pl.DeviceIdType.MESH,
        )

    def state_fwd(k):
        at = pl.ds(mul(k, fine), fine)
        return pltpu.make_async_remote_copy(
            src_ref=x.at[1, at, :],
            dst_ref=x.at[3, at, :],
            send_sem=fwd_send.at[0, k],
            recv_sem=fwd_recv.at[0, k],
            device_id={"ch": across},
            device_id_type=pl.DeviceIdType.MESH,
        )

    def last_step(c, h):
        h = lax.fori_loop(c * (fine // BLOCK), (c + 1) * (fine // BLOCK), last_block, h)
        at = sides(lax.div(c, 2), lax.rem(c, 2))
        for tile in range(subs):
            values = ubuf[pl.ds(c * fine * subs + tile, fine, stride=subs), :]
            x[0, at, tile * LANES : (tile + 1) * LANES] = values.astype(BF16)
        state_copy(lax.div(c, 2), lax.rem(c, 2) == mine).start()
        return h

    lax.fori_loop(0, FINE, last_step, state)
    lax.fori_loop(0, chips, mate_wait, 0)

    def w_part(side, slot, cols):
        return wo[side, pl.ds(mul(sources[slot], width), width), cols]

    def held(k, side, tile):
        return pl.ds(pl.multiple_of(((k * 2 + side) * subs + tile) * 2 * fine, 2 * fine), 2 * fine)

    def held_half(k, side, tile):
        low = ((lax.div(k, 2) * 2 + side) * subs + tile) * 2 * fine + lax.rem(k, 2) * fine
        return pl.ds(pl.multiple_of(low, fine), fine)

    def near_out(k, carry):
        for e in range(2):
            state_copy(2 * k + e, False).wait_recv()
            state_fwd(2 * k + e).start()
        for e in range(2):
            state_copy(2 * k + e, True).wait_recv()
        own = pl.ds(pl.multiple_of(mine * (rows // 2) + k * 2 * fine, 2 * fine), 2 * fine)
        at = pl.ds(mul(k, 2 * fine), 2 * fine)

        def tile_step(n, inner):
            cols = pl.ds(mul(n, size), size)
            for side in range(2):
                total = jnp.dot(x[0, own, :], w_part(side, 0, cols), preferred_element_type=F32)
                total += jnp.dot(x[1, at, :], w_part(side, 1, cols), preferred_element_type=F32)
                total += jnp.dot(x[2, at, :], w_part(side, 2, cols), preferred_element_type=F32)
                for p in range(size // LANES):
                    cbuf[held(k, side, n * (size // LANES) + p), :] = total[:, p * LANES : (p + 1) * LANES]
            return inner

        lax.fori_loop(0, tiles, tile_step, 0)
        return carry

    lax.fori_loop(0, FINE // 4, near_out, 0)

    def out_copy(k):
        at = pl.ds(mul(k, fine), fine)
        to = pl.ds(mul(2 * k + mine, fine), fine)
        return pltpu.make_async_copy(w.at[0, 0, at, :], out.at[to, :], out_sem.at[k])

    def give_copy(k, half_at):
        at = pl.ds(mul(k, fine), fine)
        to = pl.ds(mul(2 * k + half_at, fine), fine)
        return pltpu.make_async_remote_copy(
            src_ref=w.at[0, 1, at, :],
            dst_ref=out.at[to, :],
            send_sem=give_send.at[k],
            recv_sem=give_recv.at[k],
            device_id={"ch": pair},
            device_id_type=pl.DeviceIdType.MESH,
        )

    def far_out(k, carry):
        state_fwd(k).wait_recv()
        at = pl.ds(mul(k, fine), fine)
        for side in (1, 0):

            def tile_step(n, inner):
                cols = pl.ds(mul(n, size), size)
                total = jnp.dot(x[3, at, :], w_part(side, 3, cols), preferred_element_type=F32)
                for p in range(size // LANES):
                    tile = n * (size // LANES) + p
                    part = total[:, p * LANES : (p + 1) * LANES] + cbuf[held_half(k, side, tile), :]
                    w[0, side, at, pl.ds(mul(tile, LANES), LANES)] = part.astype(BF16)
                return inner

            lax.fori_loop(0, tiles, tile_step, 0)
            if side == 1:
                give_copy(k, mine).start()
            else:
                out_copy(k).start()
        return carry

    lax.fori_loop(0, FINE // 2, far_out, 0)
    finish_spread()
    posted(0)
    posted(1)

    def last_waits(k, carry):
        state_copy(k, False).wait_send()
        state_copy(k, True).wait_send()
        state_fwd(k).wait_send()
        out_copy(k).wait()
        give_copy(k, mine).wait_send()
        give_copy(k, 1 - mine).wait_recv()
        return carry

    lax.fori_loop(0, FINE // 2, last_waits, 0)


def hand_over(source, target, held, sem):
    rows = source.shape[0] // PIECES

    def piece(k, way):
        at = pl.ds(k * rows, rows)
        ends = (source.at[at, :], held.at[at, :], target.at[at, :])
        return pltpu.make_async_copy(ends[way], ends[way + 1], sem.at[way, k])

    for k in range(PIECES):
        piece(k, 0).start()
    for k in range(PIECES):
        piece(k, 0).wait()
        piece(k, 1).start()
    for k in range(PIECES):
        piece(k, 1).wait()


def on_device(tokens, w_input, w_output, bias_update, bias_cand, recur_gain, start_state):
    rows, width = tokens.shape
    subs = width // LANES
    n_ctx = lax.axis_size("ctx")
    n_ch = lax.axis_size("ch")
    any_spec = pl.BlockSpec(memory_space=pl.ANY)
    vmem_spec = pl.BlockSpec(memory_space=pltpu.VMEM)
    dma = pltpu.SemaphoreType.DMA
    mixed = pl.pallas_call(
        functools.partial(kernel, n_ctx, n_ch, rows, width),
        out_shape=jax.ShapeDtypeStruct((rows, width), BF16),
        in_specs=[any_spec] * 3 + [vmem_spec] * 4,
        out_specs=any_spec,
        scratch_shapes=[
            pltpu.VMEM((4, rows, width), BF16),
            pltpu.VMEM((4, 2, width, width), BF16),
            pltpu.VMEM((2, n_ch * width, width), BF16),
            pltpu.VMEM((rows * subs, LANES), F32),
            pltpu.VMEM((rows * subs, LANES), F32),
            pltpu.VMEM((rows * subs, LANES), F32),
            pltpu.VMEM((rows * subs, LANES), F32),
            pltpu.VMEM((2, 2 * subs, LANES), F32),
            pltpu.VMEM((2, n_ctx, 2 * subs, LANES), F32),
            dma((2, FINE // 2)),
            dma((2, FINE // 2)),
            dma((2, FINE // 2)),
            dma((2, FINE // 2)),
            dma((2, 2)),
            dma((2, 2)),
            dma((2, 2)),
            dma((2, 2)),
            dma((2, SPAN, 2)),
            dma((2, SPAN, 2)),
            dma((2, SPAN, 2)),
            dma((2, SPAN, 2)),
            dma((2, n_ctx // 2)),
            dma((2, n_ctx // 2)),
            dma((FINE // 2,)),
            dma((FINE // 2,)),
            dma,
            dma,
            dma,
            dma((4,)),
            dma,
            dma((FINE // 2,)),
            dma((2, n_ctx)),
            dma((2, n_ctx)),
            pltpu.SemaphoreType.REGULAR,
        ],
        compiler_params=pltpu.CompilerParams(
            collective_id=0, has_side_effects=True, vmem_limit_bytes=61 * 1024 * 1024
        ),
        cost_estimate=pl.CostEstimate(
            flops=6 * rows * width * width * n_ch,
            bytes_accessed=2 * (2 * rows * width + 3 * width * width * n_ch),
            transcendentals=4 * rows * width,
        ),
    )(
        tokens,
        w_input,
        w_output,
        bias_update.reshape(1, width),
        bias_cand.reshape(1, width),
        recur_gain.reshape(subs, LANES),
        start_state.reshape(subs, LANES),
    )
    return pl.pallas_call(
        hand_over,
        out_shape=jax.ShapeDtypeStruct((rows, width), BF16),
        in_specs=[any_spec],
        out_specs=any_spec,
        scratch_shapes=[pltpu.VMEM((rows, width), BF16), dma((2, PIECES))],
    )(mixed)


def solution(mesh):
    return jax.shard_map(
        on_device,
        mesh=mesh,
        in_specs=(
            P("ctx", "ch"),
            P(None, None, "ch"),
            P("ctx", "ch"),
            P("ch"),
            P("ch"),
            P("ch"),
            P("ch"),
        ),
        out_specs=P("ctx", "ch"),
        check_vma=False,
    )
```

```python
import functools

import jax
import jax.numpy as jnp
from jax import lax
from jax.experimental import pallas as pl
from jax.experimental.pallas import tpu as pltpu
from jax.sharding import PartitionSpec as P

LANES = 128
CHUNKS = 4
FINE = 16
PIECES = 8
TILE = 1024
BLOCK = 32
SPAN = 4
F32 = jnp.float32
BF16 = jnp.bfloat16


def mul(index, size):
    return pl.multiple_of(index * size, size)


def kernel(
    n_ctx, n_ch, rows, width,
    tok, w_in, w_out, bias_u, bias_c, gain_ref, start_ref, out,
    x, w, wo, ubuf, cbuf, sbuf, obuf, msg, inbox,
    own_send, own_recv, fwd_send, fwd_recv,
    line_send, line_recv, hop_send, hop_recv,
    row_send, row_recv, turn_send, turn_recv,
    mate_send, mate_recv, give_send, give_recv, cross_send, cross_recv,
    x_sem, w_sem, wo_sem, out_sem, msg_send, msg_recv, free,
):
    subs = width // LANES
    size = min(TILE, width)
    me = lax.axis_index("ctx")
    col = lax.axis_index("ch")
    pair = col + 1 - 2 * lax.rem(col, 2)
    across = n_ch - 1 - col
    far = lax.rem(col + 2, n_ch)
    sources = (col, pair, across, far)
    mine = lax.rem(lax.div(col + 1, 2), 2)
    chunk = rows // CHUNKS
    fine = rows // FINE
    pieces = [(k * chunk, chunk, chunk * 7 // 16) for k in range(CHUNKS - 1)]
    pieces += [(rows - chunk, chunk // 2, chunk // 4), (rows - chunk // 2, chunk // 2, chunk * 3 // 16)]
    wo_rows = w_out.shape[0]
    chips = n_ctx // 2
    core = lax.rem(me, 2)
    mate = me + 1 - 2 * core
    tiles = width // size
    y_at = lax.div(me, 2 * SPAN)
    z_at = lax.rem(lax.div(me, 2), SPAN)

    def spot(f, first, second):
        first = lax.rem(first + SPAN, SPAN)
        second = lax.rem(second + SPAN, SPAN)
        y, z = (first, second) if f == 0 else (second, first)
        return (y * SPAN + z) * 2 + core

    barrier = pltpu.get_barrier_semaphore()
    for neighbour in (pair, across):
        pl.semaphore_signal(barrier, inc=1, device_id={"ch": neighbour}, device_id_type=pl.DeviceIdType.MESH)
    around = [spot(0, y_at + 1, z_at), spot(0, y_at - 1, z_at), spot(0, y_at, z_at + 1), spot(0, y_at, z_at - 1), mate]
    for neighbour in around:
        pl.semaphore_signal(barrier, inc=1, device_id={"ctx": neighbour}, device_id_type=pl.DeviceIdType.MESH)
    pl.semaphore_wait(barrier, 2 + len(around))

    def wo_piece(owner, low, count):
        return wo.at[:, pl.ds(pl.multiple_of(owner * wo_rows + low, 16), count), :]

    wo_copy = pltpu.make_async_copy(w_out, wo.at[0, pl.ds(mul(me, wo_rows), wo_rows), :], wo_sem)
    wo_copy.start()
    cross = pltpu.make_async_remote_copy(
        src_ref=w_out,
        dst_ref=wo.at[1, pl.ds(mul(me, wo_rows), wo_rows), :],
        send_sem=cross_send,
        recv_sem=cross_recv,
        device_id={"ch": pair},
        device_id_type=pl.DeviceIdType.MESH,
    )
    cross.start()

    def own_copy(source, way, k):
        low, count, _ = pieces[k]
        peer = (pair, across)[way]
        return pltpu.make_async_remote_copy(
            src_ref=source.at[pl.ds(low, count), :],
            dst_ref=x.at[1 + way, pl.ds(low, count), :],
            send_sem=own_send.at[way, k],
            recv_sem=own_recv.at[way, k],
            device_id={"ch": peer},
            device_id_type=pl.DeviceIdType.MESH,
        )

    def fwd_copy(way, k):
        low, count, share = pieces[k]
        peer = (across, pair)[way]
        at = pl.ds(low, count - share) if way == 0 else pl.ds(low + count - share, share)
        return pltpu.make_async_remote_copy(
            src_ref=x.at[1 + way, at, :],
            dst_ref=x.at[3, at, :],
            send_sem=fwd_send.at[way, k],
            recv_sem=fwd_recv.at[way, k],
            device_id={"ch": peer},
            device_id_type=pl.DeviceIdType.MESH,
        )

    def pass_on(k):
        for way in range(2):
            own_copy(tok, way, k).wait_recv()
            fwd_copy(way, k).start()

    def await_far(k):
        for way in range(2):
            fwd_copy(way, k).wait_recv()

    for k in range(len(pieces)):
        for way in range(2):
            own_copy(tok, way, k).start()

    x_copy = pltpu.make_async_copy(tok, x.at[0], x_sem)
    x_copy.start()

    def w_copy(slot):
        return pltpu.make_async_copy(
            w_in.at[:, pl.ds(mul(sources[slot], width), width), :], w.at[slot], w_sem.at[slot]
        )

    for slot in range(4):
        w_copy(slot).start()

    half = wo_rows // 2
    quarter = half // 2

    def line_copy(f, way):
        a, b = (y_at, z_at) if f == 0 else (z_at, y_at)
        step = 1 - 2 * way
        piece = wo_piece(me, f * half, half)
        return pltpu.make_async_remote_copy(
            src_ref=piece, dst_ref=piece,
            send_sem=line_send.at[f, way], recv_sem=line_recv.at[f, way],
            device_id={"ctx": spot(f, a + step, b)}, device_id_type=pl.DeviceIdType.MESH,
        )

    def hop_copy(f, way):
        a, b = (y_at, z_at) if f == 0 else (z_at, y_at)
        step = 1 - 2 * way
        piece = wo_piece(spot(f, a - step, b), f * half + way * quarter, quarter)
        return pltpu.make_async_remote_copy(
            src_ref=piece, dst_ref=piece,
            send_sem=hop_send.at[f, way], recv_sem=hop_recv.at[f, way],
            device_id={"ctx": spot(f, a + step, b)}, device_id_type=pl.DeviceIdType.MESH,
        )

    def row_copy(f, j, way):
        a, b = (y_at, z_at) if f == 0 else (z_at, y_at)
        step = 1 - 2 * way
        piece = wo_piece(spot(f, a + j, b), f * half, half)
        return pltpu.make_async_remote_copy(
            src_ref=piece, dst_ref=piece,
            send_sem=row_send.at[f, j, way], recv_sem=row_recv.at[f, j, way],
            device_id={"ctx": spot(f, a, b + step)}, device_id_type=pl.DeviceIdType.MESH,
        )

    def turn_copy(f, j, way):
        a, b = (y_at, z_at) if f == 0 else (z_at, y_at)
        step = 1 - 2 * way
        piece = wo_piece(spot(f, a + j, b - step), f * half + way * quarter, quarter)
        return pltpu.make_async_remote_copy(
            src_ref=piece, dst_ref=piece,
            send_sem=turn_send.at[f, j, way], recv_sem=turn_recv.at[f, j, way],
            device_id={"ctx": spot(f, a, b + step)}, device_id_type=pl.DeviceIdType.MESH,
        )

    def mate_copy(f, owner):
        piece = wo_piece(owner, f * half, half)
        return pltpu.make_async_remote_copy(
            src_ref=piece, dst_ref=piece,
            send_sem=mate_send.at[f, lax.div(owner, 2)], recv_sem=mate_recv.at[f, lax.div(owner, 2)],
            device_id={"ctx": mate}, device_id_type=pl.DeviceIdType.MESH,
        )

    def share(f, first, second):
        a, b = (y_at, z_at) if f == 0 else (z_at, y_at)
        mate_copy(f, spot(f, a + first, b + second)).start()

    both = [(f, way) for f in range(2) for way in range(2)]

    def begin_lines():
        wo_copy.wait()
        cross.wait_recv()
        for f, way in both:
            line_copy(f, way).start()
        for f, way in both:
            row_copy(f, 0, way).start()
        for f in range(2):
            share(f, 0, 0)

    def begin_hops():
        for f, way in both:
            line_copy(f, way).wait_recv()
            hop_copy(f, way).start()
        for j in (1, 3):
            for f, way in both:
                row_copy(f, j, way).start()
        for j in (1, 3):
            for f in range(2):
                share(f, j, 0)

    def begin_last_row():
        for f, way in both:
            hop_copy(f, way).wait_recv()
        for f, way in both:
            row_copy(f, 2, way).start()
        for f in range(2):
            share(f, 2, 0)

    def turn(j):
        for f, way in both:
            row_copy(f, j, way).wait_recv()
            turn_copy(f, j, way).start()
        for f, way in both:
            share(f, j, 2 * way - 1)

    def turned(j):
        for f, way in both:
            turn_copy(f, j, way).wait_recv()
        for f in range(2):
            share(f, j, 2)

    def finish_spread():
        cross.wait_send()
        for f, way in both:
            line_copy(f, way).wait_send()
            hop_copy(f, way).wait_send()
        for j in range(SPAN):
            for f, way in both:
                row_copy(f, j, way).wait_send()
                turn_copy(f, j, way).wait_send()

        def done(j, carry):
            for f in range(2):
                mate_copy(f, 2 * j + core).wait_send()
            return carry

        lax.fori_loop(0, chips, done, 0)

    def mate_wait(j, carry):
        for f in range(2):
            mate_copy(f, 2 * j + 1 - core).wait_recv()
        return carry

    def natural(k, tile):
        low, count, _ = pieces[k]
        return pl.ds(pl.multiple_of(low * subs + tile * count, count), count)

    def near_gates(k):
        at = pl.ds(pieces[k][0], pieces[k][1])

        def tile_step(n, inner):
            cols = pl.ds(mul(n, size), size)
            for gate, target in ((0, sbuf), (1, obuf)):
                total = jnp.dot(x[0, at, :], w[0, gate, :, cols], preferred_element_type=F32)
                total += jnp.dot(x[1, at, :], w[1, gate, :, cols], preferred_element_type=F32)
                total += jnp.dot(x[2, at, :], w[2, gate, :, cols], preferred_element_type=F32)
                for p in range(size // LANES):
                    target[natural(k, n * (size // LANES) + p), :] = total[:, p * LANES : (p + 1) * LANES]
            return inner

        lax.fori_loop(0, tiles, tile_step, 0)

    x_copy.wait()
    for slot in range(4):
        w_copy(slot).wait()
    begin_lines()
    for k in range(len(pieces)):
        pass_on(k)
        if k == 0:
            begin_hops()
        elif k == 1:
            begin_last_row()
            turn(0)
        elif k == 2:
            turn(1)
            turn(3)
        elif k == 3:
            turn(2)
        near_gates(k)

    gain = gain_ref[...]
    start = start_ref[...]
    first_prev = jnp.where(me == 0, start, jnp.zeros_like(start))

    def far_gates(k):
        await_far(k)
        low, count, _ = pieces[k]
        at = pl.ds(low, count)

        def tile_step(n, inner):
            cols = pl.ds(mul(n, size), size)
            for gate, base, bias, target in ((0, sbuf, bias_u, ubuf), (1, obuf, bias_c, cbuf)):
                total = jnp.dot(x[3, at, :], w[3, gate, :, cols], preferred_element_type=F32)
                for p in range(size // LANES):
                    tile = n * (size // LANES) + p
                    part = total[:, p * LANES : (p + 1) * LANES] + base[natural(k, tile), :]
                    part = part + bias[:, pl.ds(mul(tile, LANES), LANES)]
                    part = part.astype(BF16).astype(F32)
                    if gate == 0:
                        part = 1.0 / (1.0 + jnp.exp(-part))
                    target[pl.ds(low * subs + tile, count, stride=subs), :] = part
            return inner

        lax.fori_loop(0, tiles, tile_step, 0)

    def token(ref, t):
        return ref[pl.ds(mul(t, subs), subs), :]

    def put(ref, t, value):
        ref[pl.ds(mul(t, subs), subs), :] = value

    def first_block(b, carry):
        acc_s, acc_o = carry
        base = b * BLOCK
        lead = jnp.where(b == 0, first_prev, jnp.zeros_like(start))
        for i in range(BLOCK):
            update = token(ubuf, base + i)
            cand = token(cbuf, base + i)
            keep = 1.0 - update
            if i == 0:
                squashed = jnp.tanh(cand + gain * lead)
                slope = keep + update * gain * (1.0 - squashed * squashed)
                offset = keep * lead + update * squashed - slope * lead
            else:
                squashed = jnp.tanh(cand)
                slope = keep + update * gain * (1.0 - squashed * squashed)
                offset = update * squashed
            put(sbuf, base + i, slope)
            put(obuf, base + i, offset)
            acc_o = slope * acc_o + offset
            acc_s = slope * acc_s
        return acc_s, acc_o

    def far_step(k, carry):
        far_gates(k)
        low, count, _ = pieces[k]
        return lax.fori_loop(low // BLOCK, (low + count) // BLOCK, first_block, carry)

    ident = (jnp.ones_like(start), jnp.zeros_like(start))
    carry = ident
    for k in range(len(pieces)):
        carry = far_step(k, carry)
        if k < 2:
            turned((0, 1)[k])
            turned((3, 2)[k])

    def message(stage_no, source, target):
        return pltpu.make_async_remote_copy(
            src_ref=msg.at[stage_no],
            dst_ref=inbox.at[stage_no, source],
            send_sem=msg_send.at[stage_no, target],
            recv_sem=msg_recv.at[stage_no, source],
            device_id={"ctx": target},
            device_id_type=pl.DeviceIdType.MESH,
        )

    def send_maps(stage_no, maps):
        msg[stage_no, pl.ds(0, subs), :] = maps[0]
        msg[stage_no, pl.ds(subs, subs), :] = maps[1]

        def post(d, c):
            message(stage_no, me, d).start()
            return c

        lax.fori_loop(me + 1, n_ctx, post, 0)

    def entering(stage_no):
        def take(d, h):
            message(stage_no, d, d).wait_recv()
            return inbox[stage_no, d, pl.ds(0, subs), :] * h + inbox[stage_no, d, pl.ds(subs, subs), :]

        return lax.fori_loop(0, me, take, start)

    def posted(stage_no):
        def done(d, c):
            message(stage_no, me, d).wait_send()
            return c

        lax.fori_loop(me + 1, n_ctx, done, 0)

    send_maps(0, carry)
    for k in range(len(pieces)):
        for way in range(2):
            own_copy(tok, way, k).wait_send()
            fwd_copy(way, k).wait_send()
    for neighbour in (pair, across):
        pl.semaphore_signal(free, inc=1, device_id={"ch": neighbour}, device_id_type=pl.DeviceIdType.MESH)
    state = entering(0)

    def second_block(b, carry):
        h, acc_s, acc_o = carry
        base = b * BLOCK
        for i in range(BLOCK):
            prev = h
            h = token(sbuf, base + i) * h + token(obuf, base + i)
            update = token(ubuf, base + i)
            cand = token(cbuf, base + i)
            keep = 1.0 - update
            squashed = jnp.tanh(cand + gain * prev)
            bend = update * gain * (1.0 - squashed * squashed)
            slope = keep + bend
            offset = update * squashed - bend * prev
            put(sbuf, base + i, slope)
            put(obuf, base + i, offset)
            acc_o = slope * acc_o + offset
            acc_s = slope * acc_s
        return h, acc_s, acc_o

    final = lax.fori_loop(0, rows // BLOCK, second_block, (state,) + ident)
    send_maps(1, final[1:])
    state = entering(1)
    pl.semaphore_wait(free, 2)

    def last_block(b, h):
        base = b * BLOCK
        for i in range(BLOCK):
            h = token(sbuf, base + i) * h + token(obuf, base + i)
            put(ubuf, base + i, h)
        return h

    def sides(k, which):
        return pl.ds(pl.multiple_of(which * (rows // 2) + k * fine, fine), fine)

    def state_copy(k, goes_across):
        slot = jnp.where(goes_across, 1, 0)
        return pltpu.make_async_remote_copy(
            src_ref=x.at[0, sides(k, jnp.where(goes_across, mine, 1 - mine)), :],
            dst_ref=x.at[1 + slot, pl.ds(mul(k, fine), fine), :],
            send_sem=own_send.at[slot, k],
            recv_sem=own_recv.at[slot, k],
            device_id={"ch": jnp.where(goes_across, across, pair)},
            device_id_type=pl.DeviceIdType.MESH,
        )

    def state_fwd(k):
        at = pl.ds(mul(k, fine), fine)
        return pltpu.make_async_remote_copy(
            src_ref=x.at[1, at, :],
            dst_ref=x.at[3, at, :],
            send_sem=fwd_send.at[0, k],
            recv_sem=fwd_recv.at[0, k],
            device_id={"ch": across},
            device_id_type=pl.DeviceIdType.MESH,
        )

    def last_step(c, h):
        h = lax.fori_loop(c * (fine // BLOCK), (c + 1) * (fine // BLOCK), last_block, h)
        at = sides(lax.div(c, 2), lax.rem(c, 2))
        for tile in range(subs):
            values = ubuf[pl.ds(c * fine * subs + tile, fine, stride=subs), :]
            x[0, at, tile * LANES : (tile + 1) * LANES] = values.astype(BF16)
        state_copy(lax.div(c, 2), lax.rem(c, 2) == mine).start()
        return h

    lax.fori_loop(0, FINE, last_step, state)
    lax.fori_loop(0, chips, mate_wait, 0)

    def w_part(side, slot, cols):
        return wo[side, pl.ds(mul(sources[slot], width), width), cols]

    def held(k, side, tile):
        return pl.ds(pl.multiple_of(((k * 2 + side) * subs + tile) * 2 * fine, 2 * fine), 2 * fine)

    def held_half(k, side, tile):
        low = ((lax.div(k, 2) * 2 + side) * subs + tile) * 2 * fine + lax.rem(k, 2) * fine
        return pl.ds(pl.multiple_of(low, fine), fine)

    def near_out(k, carry):
        for e in range(2):
            state_copy(2 * k + e, False).wait_recv()
            state_fwd(2 * k + e).start()
        for e in range(2):
            state_copy(2 * k + e, True).wait_recv()
        own = pl.ds(pl.multiple_of(mine * (rows // 2) + k * 2 * fine, 2 * fine), 2 * fine)
        at = pl.ds(mul(k, 2 * fine), 2 * fine)

        def tile_step(n, inner):
            cols = pl.ds(mul(n, size), size)
            for side in range(2):
                total = jnp.dot(x[0, own, :], w_part(side, 0, cols), preferred_element_type=F32)
                total += jnp.dot(x[1, at, :], w_part(side, 1, cols), preferred_element_type=F32)
                total += jnp.dot(x[2, at, :], w_part(side, 2, cols), preferred_element_type=F32)
                for p in range(size // LANES):
                    cbuf[held(k, side, n * (size // LANES) + p), :] = total[:, p * LANES : (p + 1) * LANES]
            return inner

        lax.fori_loop(0, tiles, tile_step, 0)
        return carry

    lax.fori_loop(0, FINE // 4, near_out, 0)

    def out_copy(k):
        at = pl.ds(mul(k, fine), fine)
        to = pl.ds(mul(2 * k + mine, fine), fine)
        return pltpu.make_async_copy(w.at[0, 0, at, :], out.at[to, :], out_sem.at[k])

    def give_copy(k, half_at):
        at = pl.ds(mul(k, fine), fine)
        to = pl.ds(mul(2 * k + half_at, fine), fine)
        return pltpu.make_async_remote_copy(
            src_ref=w.at[0, 1, at, :],
            dst_ref=out.at[to, :],
            send_sem=give_send.at[k],
            recv_sem=give_recv.at[k],
            device_id={"ch": pair},
            device_id_type=pl.DeviceIdType.MESH,
        )

    def far_out(k, carry):
        state_fwd(k).wait_recv()
        at = pl.ds(mul(k, fine), fine)
        for side in (1, 0):

            def tile_step(n, inner):
                cols = pl.ds(mul(n, size), size)
                total = jnp.dot(x[3, at, :], w_part(side, 3, cols), preferred_element_type=F32)
                for p in range(size // LANES):
                    tile = n * (size // LANES) + p
                    part = total[:, p * LANES : (p + 1) * LANES] + cbuf[held_half(k, side, tile), :]
                    w[0, side, at, pl.ds(mul(tile, LANES), LANES)] = part.astype(BF16)
                return inner

            lax.fori_loop(0, tiles, tile_step, 0)
            if side == 1:
                give_copy(k, mine).start()
            else:
                out_copy(k).start()
        return carry

    lax.fori_loop(0, FINE // 2, far_out, 0)
    finish_spread()
    posted(0)
    posted(1)

    def last_waits(k, carry):
        state_copy(k, False).wait_send()
        state_copy(k, True).wait_send()
        state_fwd(k).wait_send()
        out_copy(k).wait()
        give_copy(k, mine).wait_send()
        give_copy(k, 1 - mine).wait_recv()
        return carry

    lax.fori_loop(0, FINE // 2, last_waits, 0)


def hand_over(source, target, held, sem):
    rows = source.shape[0] // PIECES

    def piece(k, way):
        at = pl.ds(k * rows, rows)
        ends = (source.at[at, :], held.at[at, :], target.at[at, :])
        return pltpu.make_async_copy(ends[way], ends[way + 1], sem.at[way, k])

    for k in range(PIECES):
        piece(k, 0).start()
    for k in range(PIECES):
        piece(k, 0).wait()
        piece(k, 1).start()
    for k in range(PIECES):
        piece(k, 1).wait()


def on_device(tokens, w_input, w_output, bias_update, bias_cand, recur_gain, start_state):
    rows, width = tokens.shape
    subs = width // LANES
    n_ctx = lax.axis_size("ctx")
    n_ch = lax.axis_size("ch")
    any_spec = pl.BlockSpec(memory_space=pl.ANY)
    vmem_spec = pl.BlockSpec(memory_space=pltpu.VMEM)
    dma = pltpu.SemaphoreType.DMA
    mixed = pl.pallas_call(
        functools.partial(kernel, n_ctx, n_ch, rows, width),
        out_shape=jax.ShapeDtypeStruct((rows, width), BF16),
        in_specs=[any_spec] * 3 + [vmem_spec] * 4,
        out_specs=any_spec,
        scratch_shapes=[
            pltpu.VMEM((4, rows, width), BF16),
            pltpu.VMEM((4, 2, width, width), BF16),
            pltpu.VMEM((2, n_ch * width, width), BF16),
            pltpu.VMEM((rows * subs, LANES), F32),
            pltpu.VMEM((rows * subs, LANES), F32),
            pltpu.VMEM((rows * subs, LANES), F32),
            pltpu.VMEM((rows * subs, LANES), F32),
            pltpu.VMEM((2, 2 * subs, LANES), F32),
            pltpu.VMEM((2, n_ctx, 2 * subs, LANES), F32),
            dma((2, FINE // 2)),
            dma((2, FINE // 2)),
            dma((2, FINE // 2)),
            dma((2, FINE // 2)),
            dma((2, 2)),
            dma((2, 2)),
            dma((2, 2)),
            dma((2, 2)),
            dma((2, SPAN, 2)),
            dma((2, SPAN, 2)),
            dma((2, SPAN, 2)),
            dma((2, SPAN, 2)),
            dma((2, n_ctx // 2)),
            dma((2, n_ctx // 2)),
            dma((FINE // 2,)),
            dma((FINE // 2,)),
            dma,
            dma,
            dma,
            dma((4,)),
            dma,
            dma((FINE // 2,)),
            dma((2, n_ctx)),
            dma((2, n_ctx)),
            pltpu.SemaphoreType.REGULAR,
        ],
        compiler_params=pltpu.CompilerParams(
            collective_id=0, has_side_effects=True, vmem_limit_bytes=61 * 1024 * 1024
        ),
        cost_estimate=pl.CostEstimate(
            flops=6 * rows * width * width * n_ch,
            bytes_accessed=2 * (2 * rows * width + 3 * width * width * n_ch),
            transcendentals=4 * rows * width,
        ),
    )(
        tokens,
        w_input,
        w_output,
        bias_update.reshape(1, width),
        bias_cand.reshape(1, width),
        recur_gain.reshape(subs, LANES),
        start_state.reshape(subs, LANES),
    )
    return pl.pallas_call(
        hand_over,
        out_shape=jax.ShapeDtypeStruct((rows, width), BF16),
        in_specs=[any_spec],
        out_specs=any_spec,
        scratch_shapes=[pltpu.VMEM((rows, width), BF16), dma((2, PIECES))],
    )(mixed)


def solution(mesh):
    return jax.shard_map(
        on_device,
        mesh=mesh,
        in_specs=(
            P("ctx", "ch"),
            P(None, None, "ch"),
            P("ctx", "ch"),
            P("ch"),
            P("ch"),
            P("ch"),
            P("ch"),
        ),
        out_specs=P("ctx", "ch"),
        check_vma=False,
    )
```

```python
import functools

import jax
import jax.numpy as jnp
from jax import lax
from jax.experimental import pallas as pl
from jax.experimental.pallas import tpu as pltpu
from jax.sharding import PartitionSpec as P

LANES = 128
CHUNKS = 4
FINE = 16
PIECES = 8
TILE = 1024
BLOCK = 32
SPAN = 4
F32 = jnp.float32
BF16 = jnp.bfloat16


def mul(index, size):
    return pl.multiple_of(index * size, size)


def kernel(
    n_ctx, n_ch, rows, width,
    tok, w_in, w_out, bias_u, bias_c, gain_ref, start_ref, out,
    x, w, wo, ubuf, cbuf, sbuf, obuf, msg, inbox,
    own_send, own_recv, fwd_send, fwd_recv,
    line_send, line_recv, hop_send, hop_recv,
    row_send, row_recv, turn_send, turn_recv,
    mate_send, mate_recv, give_send, give_recv, cross_send, cross_recv,
    x_sem, w_sem, wo_sem, out_sem, msg_send, msg_recv, free,
):
    subs = width // LANES
    size = min(TILE, width)
    me = lax.axis_index("ctx")
    col = lax.axis_index("ch")
    pair = col + 1 - 2 * lax.rem(col, 2)
    across = n_ch - 1 - col
    far = lax.rem(col + 2, n_ch)
    sources = (col, pair, across, far)
    mine = lax.rem(lax.div(col + 1, 2), 2)
    chunk = rows // CHUNKS
    fine = rows // FINE
    pieces = [(k * chunk, chunk, chunk * 7 // 16) for k in range(CHUNKS - 1)]
    pieces += [(rows - chunk, chunk // 2, chunk // 4), (rows - chunk // 2, chunk // 2, chunk * 3 // 16)]
    wo_rows = w_out.shape[0]
    chips = n_ctx // 2
    core = lax.rem(me, 2)
    mate = me + 1 - 2 * core
    tiles = width // size
    y_at = lax.div(me, 2 * SPAN)
    z_at = lax.rem(lax.div(me, 2), SPAN)

    def spot(f, first, second):
        first = lax.rem(first + SPAN, SPAN)
        second = lax.rem(second + SPAN, SPAN)
        y, z = (first, second) if f == 0 else (second, first)
        return (y * SPAN + z) * 2 + core

    barrier = pltpu.get_barrier_semaphore()
    for neighbour in (pair, across):
        pl.semaphore_signal(barrier, inc=1, device_id={"ch": neighbour}, device_id_type=pl.DeviceIdType.MESH)
    around = [spot(0, y_at + 1, z_at), spot(0, y_at - 1, z_at), spot(0, y_at, z_at + 1), spot(0, y_at, z_at - 1), mate]
    for neighbour in around:
        pl.semaphore_signal(barrier, inc=1, device_id={"ctx": neighbour}, device_id_type=pl.DeviceIdType.MESH)
    pl.semaphore_wait(barrier, 2 + len(around))

    def wo_piece(owner, low, count):
        return wo.at[:, pl.ds(pl.multiple_of(owner * wo_rows + low, 16), count), :]

    wo_copy = pltpu.make_async_copy(w_out, wo.at[0, pl.ds(mul(me, wo_rows), wo_rows), :], wo_sem)
    wo_copy.start()
    cross = pltpu.make_async_remote_copy(
        src_ref=w_out,
        dst_ref=wo.at[1, pl.ds(mul(me, wo_rows), wo_rows), :],
        send_sem=cross_send,
        recv_sem=cross_recv,
        device_id={"ch": pair},
        device_id_type=pl.DeviceIdType.MESH,
    )
    cross.start()

    def own_copy(source, way, k):
        low, count, _ = pieces[k]
        peer = (pair, across)[way]
        return pltpu.make_async_remote_copy(
            src_ref=source.at[pl.ds(low, count), :],
            dst_ref=x.at[1 + way, pl.ds(low, count), :],
            send_sem=own_send.at[way, k],
            recv_sem=own_recv.at[way, k],
            device_id={"ch": peer},
            device_id_type=pl.DeviceIdType.MESH,
        )

    def fwd_copy(way, k):
        low, count, share = pieces[k]
        peer = (across, pair)[way]
        at = pl.ds(low, count - share) if way == 0 else pl.ds(low + count - share, share)
        return pltpu.make_async_remote_copy(
            src_ref=x.at[1 + way, at, :],
            dst_ref=x.at[3, at, :],
            send_sem=fwd_send.at[way, k],
            recv_sem=fwd_recv.at[way, k],
            device_id={"ch": peer},
            device_id_type=pl.DeviceIdType.MESH,
        )

    def pass_on(k):
        for way in range(2):
            own_copy(tok, way, k).wait_recv()
            fwd_copy(way, k).start()

    def await_far(k):
        for way in range(2):
            fwd_copy(way, k).wait_recv()

    for k in range(len(pieces)):
        for way in range(2):
            own_copy(tok, way, k).start()

    x_copy = pltpu.make_async_copy(tok, x.at[0], x_sem)
    x_copy.start()

    def w_copy(slot):
        return pltpu.make_async_copy(
            w_in.at[:, pl.ds(mul(sources[slot], width), width), :], w.at[slot], w_sem.at[slot]
        )

    for slot in range(4):
        w_copy(slot).start()

    half = wo_rows // 2
    quarter = half // 2

    def line_copy(f, way):
        a, b = (y_at, z_at) if f == 0 else (z_at, y_at)
        step = 1 - 2 * way
        piece = wo_piece(me, f * half, half)
        return pltpu.make_async_remote_copy(
            src_ref=piece, dst_ref=piece,
            send_sem=line_send.at[f, way], recv_sem=line_recv.at[f, way],
            device_id={"ctx": spot(f, a + step, b)}, device_id_type=pl.DeviceIdType.MESH,
        )

    def hop_copy(f, way):
        a, b = (y_at, z_at) if f == 0 else (z_at, y_at)
        step = 1 - 2 * way
        piece = wo_piece(spot(f, a - step, b), f * half + way * quarter, quarter)
        return pltpu.make_async_remote_copy(
            src_ref=piece, dst_ref=piece,
            send_sem=hop_send.at[f, way], recv_sem=hop_recv.at[f, way],
            device_id={"ctx": spot(f, a + step, b)}, device_id_type=pl.DeviceIdType.MESH,
        )

    def row_copy(f, j, way):
        a, b = (y_at, z_at) if f == 0 else (z_at, y_at)
        step = 1 - 2 * way
        piece = wo_piece(spot(f, a + j, b), f * half, half)
        return pltpu.make_async_remote_copy(
            src_ref=piece, dst_ref=piece,
            send_sem=row_send.at[f, j, way], recv_sem=row_recv.at[f, j, way],
            device_id={"ctx": spot(f, a, b + step)}, device_id_type=pl.DeviceIdType.MESH,
        )

    def turn_copy(f, j, way):
        a, b = (y_at, z_at) if f == 0 else (z_at, y_at)
        step = 1 - 2 * way
        piece = wo_piece(spot(f, a + j, b - step), f * half + way * quarter, quarter)
        return pltpu.make_async_remote_copy(
            src_ref=piece, dst_ref=piece,
            send_sem=turn_send.at[f, j, way], recv_sem=turn_recv.at[f, j, way],
            device_id={"ctx": spot(f, a, b + step)}, device_id_type=pl.DeviceIdType.MESH,
        )

    def mate_copy(f, owner):
        piece = wo_piece(owner, f * half, half)
        return pltpu.make_async_remote_copy(
            src_ref=piece, dst_ref=piece,
            send_sem=mate_send.at[f, lax.div(owner, 2)], recv_sem=mate_recv.at[f, lax.div(owner, 2)],
            device_id={"ctx": mate}, device_id_type=pl.DeviceIdType.MESH,
        )

    def share(f, first, second):
        a, b = (y_at, z_at) if f == 0 else (z_at, y_at)
        mate_copy(f, spot(f, a + first, b + second)).start()

    both = [(f, way) for f in range(2) for way in range(2)]

    def begin_lines():
        wo_copy.wait()
        cross.wait_recv()
        for f, way in both:
            line_copy(f, way).start()
        for f, way in both:
            row_copy(f, 0, way).start()
        for f in range(2):
            share(f, 0, 0)

    def begin_hops():
        for f, way in both:
            line_copy(f, way).wait_recv()
            hop_copy(f, way).start()
        for j in (1, 3):
            for f, way in both:
                row_copy(f, j, way).start()
        for j in (1, 3):
            for f in range(2):
                share(f, j, 0)

    def begin_last_row():
        for f, way in both:
            hop_copy(f, way).wait_recv()
        for f, way in both:
            row_copy(f, 2, way).start()
        for f in range(2):
            share(f, 2, 0)

    def turn(j):
        for f, way in both:
            row_copy(f, j, way).wait_recv()
            turn_copy(f, j, way).start()
        for f, way in both:
            share(f, j, 2 * way - 1)

    def turned(j):
        for f, way in both:
            turn_copy(f, j, way).wait_recv()
        for f in range(2):
            share(f, j, 2)

    def finish_spread():
        cross.wait_send()
        for f, way in both:
            line_copy(f, way).wait_send()
            hop_copy(f, way).wait_send()
        for j in range(SPAN):
            for f, way in both:
                row_copy(f, j, way).wait_send()
                turn_copy(f, j, way).wait_send()

        def done(j, carry):
            for f in range(2):
                mate_copy(f, 2 * j + core).wait_send()
            return carry

        lax.fori_loop(0, chips, done, 0)

    def mate_wait(j, carry):
        for f in range(2):
            mate_copy(f, 2 * j + 1 - core).wait_recv()
        return carry

    def natural(k, tile):
        low, count, _ = pieces[k]
        return pl.ds(pl.multiple_of(low * subs + tile * count, count), count)

    def near_gates(k):
        at = pl.ds(pieces[k][0], pieces[k][1])

        def tile_step(n, inner):
            cols = pl.ds(mul(n, size), size)
            for gate, target in ((0, sbuf), (1, obuf)):
                total = jnp.dot(x[0, at, :], w[0, gate, :, cols], preferred_element_type=F32)
                total += jnp.dot(x[1, at, :], w[1, gate, :, cols], preferred_element_type=F32)
                total += jnp.dot(x[2, at, :], w[2, gate, :, cols], preferred_element_type=F32)
                for p in range(size // LANES):
                    target[natural(k, n * (size // LANES) + p), :] = total[:, p * LANES : (p + 1) * LANES]
            return inner

        lax.fori_loop(0, tiles, tile_step, 0)

    x_copy.wait()
    for slot in range(4):
        w_copy(slot).wait()
    begin_lines()
    for k in range(len(pieces)):
        pass_on(k)
        if k == 0:
            begin_hops()
        elif k == 1:
            begin_last_row()
            turn(0)
        elif k == 2:
            turn(1)
            turn(3)
        elif k == 3:
            turn(2)
        near_gates(k)

    gain = gain_ref[...]
    start = start_ref[...]
    first_prev = jnp.where(me == 0, start, jnp.zeros_like(start))

    def far_gates(k):
        await_far(k)
        low, count, _ = pieces[k]
        at = pl.ds(low, count)

        def tile_step(n, inner):
            cols = pl.ds(mul(n, size), size)
            for gate, base, bias, target in ((0, sbuf, bias_u, ubuf), (1, obuf, bias_c, cbuf)):
                total = jnp.dot(x[3, at, :], w[3, gate, :, cols], preferred_element_type=F32)
                for p in range(size // LANES):
                    tile = n * (size // LANES) + p
                    part = total[:, p * LANES : (p + 1) * LANES] + base[natural(k, tile), :]
                    part = part + bias[:, pl.ds(mul(tile, LANES), LANES)]
                    part = part.astype(BF16).astype(F32)
                    if gate == 0:
                        part = 1.0 / (1.0 + jnp.exp(-part))
                    target[pl.ds(low * subs + tile, count, stride=subs), :] = part
            return inner

        lax.fori_loop(0, tiles, tile_step, 0)

    def token(ref, t):
        return ref[pl.ds(mul(t, subs), subs), :]

    def put(ref, t, value):
        ref[pl.ds(mul(t, subs), subs), :] = value

    def first_block(b, carry):
        acc_s, acc_o = carry
        base = b * BLOCK
        lead = jnp.where(b == 0, first_prev, jnp.zeros_like(start))
        for i in range(BLOCK):
            update = token(ubuf, base + i)
            cand = token(cbuf, base + i)
            keep = 1.0 - update
            if i == 0:
                squashed = jnp.tanh(cand + gain * lead)
                slope = keep + update * gain * (1.0 - squashed * squashed)
                offset = keep * lead + update * squashed - slope * lead
            else:
                squashed = jnp.tanh(cand)
                slope = keep + update * gain * (1.0 - squashed * squashed)
                offset = update * squashed
            put(sbuf, base + i, slope)
            put(obuf, base + i, offset)
            acc_o = slope * acc_o + offset
            acc_s = slope * acc_s
        return acc_s, acc_o

    def far_step(k, carry):
        far_gates(k)
        low, count, _ = pieces[k]
        return lax.fori_loop(low // BLOCK, (low + count) // BLOCK, first_block, carry)

    ident = (jnp.ones_like(start), jnp.zeros_like(start))
    carry = ident
    for k in range(len(pieces)):
        carry = far_step(k, carry)
        if k < 2:
            turned((0, 1)[k])
            turned((3, 2)[k])

    def message(stage_no, source, target):
        return pltpu.make_async_remote_copy(
            src_ref=msg.at[stage_no],
            dst_ref=inbox.at[stage_no, source],
            send_sem=msg_send.at[stage_no, target],
            recv_sem=msg_recv.at[stage_no, source],
            device_id={"ctx": target},
            device_id_type=pl.DeviceIdType.MESH,
        )

    def send_maps(stage_no, maps):
        msg[stage_no, pl.ds(0, subs), :] = maps[0]
        msg[stage_no, pl.ds(subs, subs), :] = maps[1]

        def post(d, c):
            message(stage_no, me, d).start()
            return c

        lax.fori_loop(me + 1, n_ctx, post, 0)

    def entering(stage_no):
        def take(d, h):
            message(stage_no, d, d).wait_recv()
            return inbox[stage_no, d, pl.ds(0, subs), :] * h + inbox[stage_no, d, pl.ds(subs, subs), :]

        return lax.fori_loop(0, me, take, start)

    def posted(stage_no):
        def done(d, c):
            message(stage_no, me, d).wait_send()
            return c

        lax.fori_loop(me + 1, n_ctx, done, 0)

    send_maps(0, carry)
    state = entering(0)

    def second_block(b, carry):
        h, acc_s, acc_o = carry
        base = b * BLOCK
        for i in range(BLOCK):
            prev = h
            h = token(sbuf, base + i) * h + token(obuf, base + i)
            update = token(ubuf, base + i)
            cand = token(cbuf, base + i)
            keep = 1.0 - update
            squashed = jnp.tanh(cand + gain * prev)
            bend = update * gain * (1.0 - squashed * squashed)
            slope = keep + bend
            offset = update * squashed - bend * prev
            put(sbuf, base + i, slope)
            put(obuf, base + i, offset)
            acc_o = slope * acc_o + offset
            acc_s = slope * acc_s
        return h, acc_s, acc_o

    final = lax.fori_loop(0, rows // BLOCK, second_block, (state,) + ident)
    send_maps(1, final[1:])
    for k in range(len(pieces)):
        for way in range(2):
            own_copy(tok, way, k).wait_send()
            fwd_copy(way, k).wait_send()
    for neighbour in (pair, across):
        pl.semaphore_signal(free, inc=1, device_id={"ch": neighbour}, device_id_type=pl.DeviceIdType.MESH)
    lax.fori_loop(0, chips, mate_wait, 0)
    state = entering(1)
    pl.semaphore_wait(free, 2)

    def last_block(b, h):
        base = b * BLOCK
        for i in range(BLOCK):
            h = token(sbuf, base + i) * h + token(obuf, base + i)
            put(ubuf, base + i, h)
        return h

    def sides(k, which):
        return pl.ds(pl.multiple_of(which * (rows // 2) + k * fine, fine), fine)

    def state_copy(k, goes_across):
        slot = jnp.where(goes_across, 1, 0)
        return pltpu.make_async_remote_copy(
            src_ref=x.at[0, sides(k, jnp.where(goes_across, mine, 1 - mine)), :],
            dst_ref=x.at[1 + slot, pl.ds(mul(k, fine), fine), :],
            send_sem=own_send.at[slot, k],
            recv_sem=own_recv.at[slot, k],
            device_id={"ch": jnp.where(goes_across, across, pair)},
            device_id_type=pl.DeviceIdType.MESH,
        )

    def state_fwd(k):
        at = pl.ds(mul(k, fine), fine)
        return pltpu.make_async_remote_copy(
            src_ref=x.at[1, at, :],
            dst_ref=x.at[3, at, :],
            send_sem=fwd_send.at[0, k],
            recv_sem=fwd_recv.at[0, k],
            device_id={"ch": across},
            device_id_type=pl.DeviceIdType.MESH,
        )

    def last_step(c, h):
        h = lax.fori_loop(c * (fine // BLOCK), (c + 1) * (fine // BLOCK), last_block, h)
        at = sides(lax.div(c, 2), lax.rem(c, 2))
        for tile in range(subs):
            values = ubuf[pl.ds(c * fine * subs + tile, fine, stride=subs), :]
            x[0, at, tile * LANES : (tile + 1) * LANES] = values.astype(BF16)
        state_copy(lax.div(c, 2), lax.rem(c, 2) == mine).start()
        return h

    lax.fori_loop(0, FINE, last_step, state)

    def w_part(side, slot, cols):
        return wo[side, pl.ds(mul(sources[slot], width), width), cols]

    def held(k, side, tile):
        return pl.ds(pl.multiple_of(((k * 2 + side) * subs + tile) * 2 * fine, 2 * fine), 2 * fine)

    def held_half(k, side, tile):
        low = ((lax.div(k, 2) * 2 + side) * subs + tile) * 2 * fine + lax.rem(k, 2) * fine
        return pl.ds(pl.multiple_of(low, fine), fine)

    def near_out(k, carry):
        for e in range(2):
            state_copy(2 * k + e, False).wait_recv()
            state_fwd(2 * k + e).start()
        for e in range(2):
            state_copy(2 * k + e, True).wait_recv()
        own = pl.ds(pl.multiple_of(mine * (rows // 2) + k * 2 * fine, 2 * fine), 2 * fine)
        at = pl.ds(mul(k, 2 * fine), 2 * fine)

        def tile_step(n, inner):
            cols = pl.ds(mul(n, size), size)
            for side in range(2):
                total = jnp.dot(x[0, own, :], w_part(side, 0, cols), preferred_element_type=F32)
                total += jnp.dot(x[1, at, :], w_part(side, 1, cols), preferred_element_type=F32)
                total += jnp.dot(x[2, at, :], w_part(side, 2, cols), preferred_element_type=F32)
                for p in range(size // LANES):
                    cbuf[held(k, side, n * (size // LANES) + p), :] = total[:, p * LANES : (p + 1) * LANES]
            return inner

        lax.fori_loop(0, tiles, tile_step, 0)
        return carry

    lax.fori_loop(0, FINE // 4, near_out, 0)

    def out_copy(k):
        at = pl.ds(mul(k, fine), fine)
        to = pl.ds(mul(2 * k + mine, fine), fine)
        return pltpu.make_async_copy(w.at[0, 0, at, :], out.at[to, :], out_sem.at[k])

    def give_copy(k, half_at):
        at = pl.ds(mul(k, fine), fine)
        to = pl.ds(mul(2 * k + half_at, fine), fine)
        return pltpu.make_async_remote_copy(
            src_ref=w.at[0, 1, at, :],
            dst_ref=out.at[to, :],
            send_sem=give_send.at[k],
            recv_sem=give_recv.at[k],
            device_id={"ch": pair},
            device_id_type=pl.DeviceIdType.MESH,
        )

    def far_out(k, carry):
        state_fwd(k).wait_recv()
        at = pl.ds(mul(k, fine), fine)
        for side in (1, 0):

            def tile_step(n, inner):
                cols = pl.ds(mul(n, size), size)
                total = jnp.dot(x[3, at, :], w_part(side, 3, cols), preferred_element_type=F32)
                for p in range(size // LANES):
                    tile = n * (size // LANES) + p
                    part = total[:, p * LANES : (p + 1) * LANES] + cbuf[held_half(k, side, tile), :]
                    w[0, side, at, pl.ds(mul(tile, LANES), LANES)] = part.astype(BF16)
                return inner

            lax.fori_loop(0, tiles, tile_step, 0)
            if side == 1:
                give_copy(k, mine).start()
            else:
                out_copy(k).start()
        return carry

    lax.fori_loop(0, FINE // 2, far_out, 0)
    finish_spread()
    posted(0)
    posted(1)

    def last_waits(k, carry):
        state_copy(k, False).wait_send()
        state_copy(k, True).wait_send()
        state_fwd(k).wait_send()
        out_copy(k).wait()
        give_copy(k, mine).wait_send()
        give_copy(k, 1 - mine).wait_recv()
        return carry

    lax.fori_loop(0, FINE // 2, last_waits, 0)


def hand_over(source, target, held, sem):
    rows = source.shape[0] // PIECES

    def piece(k, way):
        at = pl.ds(k * rows, rows)
        ends = (source.at[at, :], held.at[at, :], target.at[at, :])
        return pltpu.make_async_copy(ends[way], ends[way + 1], sem.at[way, k])

    for k in range(PIECES):
        piece(k, 0).start()
    for k in range(PIECES):
        piece(k, 0).wait()
        piece(k, 1).start()
    for k in range(PIECES):
        piece(k, 1).wait()


def on_device(tokens, w_input, w_output, bias_update, bias_cand, recur_gain, start_state):
    rows, width = tokens.shape
    subs = width // LANES
    n_ctx = lax.axis_size("ctx")
    n_ch = lax.axis_size("ch")
    any_spec = pl.BlockSpec(memory_space=pl.ANY)
    vmem_spec = pl.BlockSpec(memory_space=pltpu.VMEM)
    dma = pltpu.SemaphoreType.DMA
    mixed = pl.pallas_call(
        functools.partial(kernel, n_ctx, n_ch, rows, width),
        out_shape=jax.ShapeDtypeStruct((rows, width), BF16),
        in_specs=[any_spec] * 3 + [vmem_spec] * 4,
        out_specs=any_spec,
        scratch_shapes=[
            pltpu.VMEM((4, rows, width), BF16),
            pltpu.VMEM((4, 2, width, width), BF16),
            pltpu.VMEM((2, n_ch * width, width), BF16),
            pltpu.VMEM((rows * subs, LANES), F32),
            pltpu.VMEM((rows * subs, LANES), F32),
            pltpu.VMEM((rows * subs, LANES), F32),
            pltpu.VMEM((rows * subs, LANES), F32),
            pltpu.VMEM((2, 2 * subs, LANES), F32),
            pltpu.VMEM((2, n_ctx, 2 * subs, LANES), F32),
            dma((2, FINE // 2)),
            dma((2, FINE // 2)),
            dma((2, FINE // 2)),
            dma((2, FINE // 2)),
            dma((2, 2)),
            dma((2, 2)),
            dma((2, 2)),
            dma((2, 2)),
            dma((2, SPAN, 2)),
            dma((2, SPAN, 2)),
            dma((2, SPAN, 2)),
            dma((2, SPAN, 2)),
            dma((2, n_ctx // 2)),
            dma((2, n_ctx // 2)),
            dma((FINE // 2,)),
            dma((FINE // 2,)),
            dma,
            dma,
            dma,
            dma((4,)),
            dma,
            dma((FINE // 2,)),
            dma((2, n_ctx)),
            dma((2, n_ctx)),
            pltpu.SemaphoreType.REGULAR,
        ],
        compiler_params=pltpu.CompilerParams(
            collective_id=0, has_side_effects=True, vmem_limit_bytes=61 * 1024 * 1024
        ),
        cost_estimate=pl.CostEstimate(
            flops=6 * rows * width * width * n_ch,
            bytes_accessed=2 * (2 * rows * width + 3 * width * width * n_ch),
            transcendentals=4 * rows * width,
        ),
    )(
        tokens,
        w_input,
        w_output,
        bias_update.reshape(1, width),
        bias_cand.reshape(1, width),
        recur_gain.reshape(subs, LANES),
        start_state.reshape(subs, LANES),
    )
    return pl.pallas_call(
        hand_over,
        out_shape=jax.ShapeDtypeStruct((rows, width), BF16),
        in_specs=[any_spec],
        out_specs=any_spec,
        scratch_shapes=[pltpu.VMEM((rows, width), BF16), dma((2, PIECES))],
    )(mixed)


def solution(mesh):
    return jax.shard_map(
        on_device,
        mesh=mesh,
        in_specs=(
            P("ctx", "ch"),
            P(None, None, "ch"),
            P("ctx", "ch"),
            P("ch"),
            P("ch"),
            P("ch"),
            P("ch"),
        ),
        out_specs=P("ctx", "ch"),
        check_vma=False,
    )
```
